512 devices in a mesh: row: 16 (over y, core), col: 32 (over x, z).
Axes of the slice: x: 4, y: 8, z: 8, core: 2. Of those that a mesh axis runs over, the one named last changes fastest.
Arguments:
- hidden_acts: bfloat16 [256, 29568], P('row', 'col'), may hold values from -6 to 6
- output_errors: bfloat16 [256, 4096], P('col', 'row'), may hold values from -6 to 6
- col_points: int32 [32], replicated, may hold values from 0 to 64, as said below
- row_points: int32 [16], replicated, may hold values from 0 to 32, as said below
- worker_mask: int32 [16, 32], replicated, may hold values from 0 to 1, as said below
Outputs:
- clipped_grad: float32 [8, 512, 29568], P(None, 'col', 'row')
The draws below stay inside these ranges and needn't reach their ends.
Inputs may be any that keep to these rules, and one draw needn't show every extreme that they name: `col_points`: distinct node indices. `row_points`: distinct node indices. `worker_mask`: each row of the grid has between 1 and 8 erased workers.
All inputs are finite; a program needn't handle non-finite values.
Results may differ from the reference program's by a relative error of at most 0.02.
Values may be sent and summed in bfloat16 or wider, within the bound.
No kernel may reach another device: no remote copies, remote signals or barrier semaphores. Data moves between devices by JAX's collectives and lax.ppermute only.
A program may use at most 128 MiB of HBM per device.

```python
import jax
import jax.numpy as jnp
from jax import lax

D = 4096
FF = 29568
TOKENS = 256
N_ROW = 16
N_COL = 32


def draw_col_points(key, part):
    return jax.random.permutation(key, 2 * N_COL + 1)[:N_COL].astype(jnp.int32)


def draw_row_points(key, part):
    return jax.random.permutation(key, 2 * N_ROW + 1)[:N_ROW].astype(jnp.int32)


def one_order(row_key):
    return jax.random.permutation(row_key, N_COL)


def draw_worker_mask(key, part):
    key_count = jax.random.fold_in(key, 11)
    key_order = jax.random.fold_in(key, 23)
    counts = jax.random.randint(key_count, (N_ROW,), 1, N_COL // 4 + 1)
    counts = jnp.where(jnp.arange(N_ROW) == 0, N_COL // 4, counts)
    orders = jax.vmap(one_order)(jax.random.split(key_order, N_ROW))
    return jnp.where(orders < counts[:, None], 0, 1).astype(jnp.int32)


def shard_levels(own_key, extent, cuts, smallest, high):
    level, own = 1.0, jax.random.fold_in(own_key, 6)
    for dim, parts in cuts:
        draws = jnp.exp(jax.random.uniform(jax.random.fold_in(own, dim), (parts,), jnp.float32, smallest / len(cuts), high / len(cuts)))
        level = level * jnp.repeat(draws, extent[dim] // parts).reshape([-1 if axis == dim else 1 for axis in range(len(extent))])
    return level


def noise(own_key, shape, spread, reach, cuts=(), dtype=jnp.bfloat16):
    factor_of = shard_levels(own_key, shape, cuts, -0.22, 0.18) if cuts else 1.0
    values = jax.random.normal(own_key, shape, jnp.float32) * spread * factor_of
    return jnp.minimum(jnp.maximum(values, -reach), reach).astype(dtype)


def setup_inputs(seed: int = 0) -> dict:
    key_list = jax.random.split(jax.random.key(seed), 6)
    return {
        "hidden_acts": noise(key_list[0], (TOKENS, FF), 1.0, 6.0, ((0, 16), (1, 32))),
        "output_errors": noise(key_list[1], (TOKENS, D), 1.0, 6.0, ((0, 32), (1, 16))),
        "col_points": draw_col_points(jax.random.fold_in(key_list[5], 71), 0),
        "row_points": draw_row_points(jax.random.fold_in(key_list[5], 71), 0),
        "worker_mask": draw_worker_mask(jax.random.fold_in(key_list[5], 71), 0),
    }


def node_value(index, count):
    return jnp.cos(jnp.pi * (2.0 * index.astype(jnp.float32) + 1.0) / (2.0 * count))

def berrut(nodes, signs, live, targets):
    terms = (live * signs)[:, None] / (targets[None, :] - nodes[:, None])
    return terms / lax.optimization_barrier(jnp.sum(terms, axis=0, keepdims=True))

def rank_signs(points, live):
    lower = (points[None, :] < points[:, None]).astype(jnp.int32)
    ranks = lax.optimization_barrier(jnp.sum(lower * live[None, :], axis=1))
    return (1 - 2 * (ranks % 2)).astype(jnp.float32)

def reference(hidden_acts, output_errors, col_points, row_points, worker_mask):
    act_blocks = N_COL // 2
    err_blocks = N_ROW // 2
    act_width = FF // act_blocks
    err_width = D // err_blocks
    data_acts = node_value(jnp.arange(act_blocks), act_blocks)
    data_errs = node_value(jnp.arange(err_blocks), err_blocks)
    work_acts = node_value(col_points, 2 * N_COL + 1)
    work_errs = node_value(row_points, 2 * N_ROW + 1)
    alt_acts = (1 - 2 * (jnp.arange(act_blocks) % 2)).astype(jnp.float32)
    alt_errs = (1 - 2 * (jnp.arange(err_blocks) % 2)).astype(jnp.float32)
    encode_acts = berrut(data_acts, alt_acts, jnp.ones((act_blocks,), jnp.float32), work_acts)
    encode_errs = berrut(data_errs, alt_errs, jnp.ones((err_blocks,), jnp.float32), work_errs)
    blocks_acts = hidden_acts.astype(jnp.float32).reshape(TOKENS, act_blocks, act_width)
    coded_acts = jnp.einsum('kj,tkf->jtf', encode_acts, blocks_acts).astype(jnp.bfloat16)
    blocks_errs = output_errors.astype(jnp.float32).reshape(TOKENS, err_blocks, err_width)
    coded_errs = jnp.einsum('li,tld->itd', encode_errs, blocks_errs).astype(jnp.bfloat16)
    all_rows = jnp.ones((N_ROW,), jnp.int32)
    decode_errs = berrut(work_errs, rank_signs(row_points, all_rows), jnp.ones((N_ROW,), jnp.float32), data_errs)
    acts_wide = coded_acts.astype(jnp.float32)

    def one_row(total, index):
        errs_here = coded_errs[index].astype(jnp.float32)
        product = jnp.einsum('td,jtf->jdf', errs_here, acts_wide).astype(jnp.bfloat16)
        live = worker_mask[index]
        decode_acts = berrut(work_acts, rank_signs(col_points, live), live.astype(jnp.float32), data_acts)
        decoded = jnp.einsum('jk,jdf->dkf', decode_acts, product.astype(jnp.float32))
        decoded = decoded.reshape(err_width, FF).astype(jnp.bfloat16)
        total = total + decode_errs[index][:, None, None] * decoded.astype(jnp.float32)[None]
        return (total, None)
    start = jnp.zeros((err_blocks, err_width, FF), jnp.float32)
    grad, unused = lax.scan(one_row, start, jnp.arange(N_ROW))
    squares = jnp.sum(grad * grad)
    factor = jnp.minimum(1.0, jnp.sqrt(jnp.float32(FF * D)) / jnp.sqrt(squares + 1e-06))
    return grad * factor
```

```python
import functools

import jax
import jax.numpy as jnp
from jax import lax
from jax.experimental import pallas as pl
from jax.experimental.pallas import tpu as pltpu
from jax.sharding import Mesh
from jax.sharding import PartitionSpec as P

D = 4096
FF = 29568
ROW = ("row_0", "row_1")
COL = ("col_0", "col_1")
ROW_Z = ("row_0", "row_1", "col_1")
N_ROW = 16
N_X = 4
N_Z = 8
N_COL = 32
HALF = FF // N_COL
WIDTH = FF // N_ROW
CHUNK = 64
SHIFT = HALF - (HALF // CHUNK) * CHUNK
BF16 = jnp.bfloat16
F32 = jnp.float32
VMEM_LIMIT = 48 * 1024 * 1024


def low_lanes(rows):
    return lax.broadcasted_iota(jnp.int32, (rows, 128), 1) < 64


def swap_halves(tile):
    return pltpu.roll(tile, 64, 1)


def pack_kernel(half_ref, acts_ref, errs_ref, out_ref, padded):
    padded[...] = jnp.zeros_like(padded)
    padded[:, :HALF] = acts_ref[...].astype(F32)
    plain = padded[...]
    acts = jnp.where(half_ref[0] == 1, pltpu.roll(plain, SHIFT, 1), plain)
    errs = errs_ref[...].astype(F32)
    low = low_lanes(8)
    lane = lax.broadcasted_iota(jnp.int32, (8, 128), 1)
    err_tiles = []
    for z in range(N_Z):
        first = pltpu.roll(errs[:, :128], (128 - 16 * z) % 128, 1)
        second = pltpu.roll(errs[:, 128:], (144 - 16 * z) % 128, 1)
        err_tiles.append(jnp.where(lane < 16, first, second))
    for row in range(N_ROW):
        lanes = slice(128 * (row // 2), 128 * (row // 2) + 128)
        upper, lower = acts[:8, lanes], acts[8:, lanes]
        if row % 2 == 0:
            tile = jnp.where(low, upper, swap_halves(lower))
        else:
            tile = jnp.where(low, swap_halves(upper), lower)
        for z in range(N_Z):
            both = jnp.concatenate([tile, err_tiles[z]], axis=0)
            out_ref[row * N_Z + z] = both.astype(BF16)


def spread_kernel(in_ref, out_ref):
    group = lax.broadcasted_iota(jnp.int32, (64, 128), 1) // 16
    for z in range(N_Z):
        acts = jnp.concatenate(
            [in_ref[row * N_Z + z].astype(F32)[:8] for row in range(N_ROW)], axis=0
        ).astype(BF16)
        for x in range(N_X):
            out_ref[x, 128 * z : 128 * z + 128, :] = acts
    for parity in range(2):
        sums = [jnp.zeros((64, 128), F32) for _ in range(2)]
        for block in range(8):
            row = 2 * block + parity
            source = jnp.concatenate(
                [
                    in_ref[row * N_Z + z].astype(F32)[8:]
                    for z in (0, 2, 4, 6, 1, 3, 5, 7)
                ],
                axis=0,
            )
            for q in range(2):
                turned = pltpu.roll(source, (128 + 16 * (block - q)) % 128, 1)
                sums[q] = jnp.where(group == block, turned, sums[q])
        for q in range(2):
            out_ref[2 * parity + q, 1024:1088, :] = sums[q].astype(BF16)


def node_value(index, count):
    return jnp.cos(jnp.pi * (2.0 * index.astype(F32) + 1.0) / (2.0 * count))


def parity_sign(count):
    return (1 - 2 * (count % 2)).astype(F32)


def mix_kernel(cols_ref, rows_ref, mask_ref, out_ref):
    iota = functools.partial(lax.broadcasted_iota, jnp.int32)
    cols = cols_ref[...]
    rows = rows_ref[...]
    live = mask_ref[...]
    col_eye = iota((N_COL, N_COL), 0) == iota((N_COL, N_COL), 1)
    row_eye = iota((N_ROW, N_ROW), 0) == iota((N_ROW, N_ROW), 1)
    col_point = jnp.sum(jnp.where(col_eye, cols, 0), axis=1, keepdims=True)
    row_point = jnp.sum(jnp.where(row_eye, rows, 0), axis=1, keepdims=True)
    work_acts = node_value(col_point, 2 * N_COL + 1)
    work_errs = node_value(row_point, 2 * N_ROW + 1)
    row_rank = jnp.sum((rows < row_point).astype(jnp.int32), axis=1, keepdims=True)
    row_sign = parity_sign(row_rank)

    lane = iota((1, 128), 1)
    err_in, act_in = lane // 16, lane % 16
    term = parity_sign(err_in) / (work_errs - node_value(err_in, 8))
    total = jnp.sum(jnp.where(act_in == 0, term, 0.0), axis=1, keepdims=True)
    encode_errs = term / total
    term = parity_sign(act_in) / (work_acts - node_value(act_in, 16))
    total = jnp.sum(jnp.where(err_in == 0, term, 0.0), axis=1, keepdims=True)
    encode_acts = term / total
    act_out, err_out = lane // 8, lane % 8
    term = row_sign / (node_value(err_out, 8) - work_errs)
    decode_errs = term / jnp.sum(term, axis=0, keepdims=True)
    inverse = 1.0 / (node_value(act_out, 16) - work_acts)

    lower = cols < col_point
    total = jnp.zeros((128, 128), F32)
    left, right = [], []
    for i in range(N_ROW):
        here = live[i : i + 1, :]
        rank = jnp.sum(jnp.where(lower, here, 0), axis=1, keepdims=True)
        own = jnp.sum(jnp.where(col_eye, here, 0), axis=1, keepdims=True)
        term = (own.astype(F32) * parity_sign(rank)) * inverse
        decode = term / jnp.sum(term, axis=0, keepdims=True)
        left.append(decode * decode_errs[i : i + 1, :])
        right.append(encode_acts * encode_errs[i : i + 1, :])
    total = lax.dot_general(
        jnp.concatenate(left, axis=0),
        jnp.concatenate(right, axis=0),
        (((0,), (0,)), ((), ())),
        preferred_element_type=F32,
        precision=lax.Precision.HIGHEST,
    )
    out_ref[...] = total


def product_kernel(in_ref, mix_ref, out_ref, squares_ref, products):
    low = low_lanes(128)
    errs = jnp.concatenate(
        [
            in_ref[x, 1024 + 32 * part : 1056 + 32 * part, :]
            for part in range(2)
            for x in range(N_X)
        ],
        axis=0,
    )
    errs = errs.astype(F32).T.astype(BF16)
    for block in range(16):
        x, z = block // 4, 2 * (block % 4)
        first = in_ref[x, 128 * z : 128 * z + 128, :].astype(F32)
        second = in_ref[x, 128 * z + 128 : 128 * z + 256, :].astype(F32)
        acts = jnp.concatenate(
            [
                jnp.where(low, first, swap_halves(second)),
                jnp.where(low, swap_halves(first), second),
            ],
            axis=0,
        ).astype(BF16)
        products[pl.ds(block, 128, stride=16), :] = jnp.dot(
            errs, acts, preferred_element_type=F32
        )
    mix = mix_ref[...].astype(BF16)
    squares = jnp.zeros((128, 128), F32)
    for pair in range(8):
        mixed = []
        for r in (2 * pair, 2 * pair + 1):
            piece = jnp.concatenate(
                [
                    products[(block * 16 + r) * 16 : (block * 16 + r) * 16 + 16, :]
                    for block in range(8)
                ],
                axis=0,
            ).astype(BF16)
            grad = jnp.dot(mix, piece, preferred_element_type=F32)
            squares = squares + grad * grad
            mixed.append(grad)
        for k in range(N_ROW):
            both = jnp.concatenate(
                [grad[8 * k : 8 * k + 8, :] for grad in mixed], axis=0
            )
            out_ref[k, 16 * pair : 16 * pair + 16, :] = both.astype(BF16)
    squares_ref[...] = jnp.sum(squares.reshape(16, 8, 128), axis=0)


def place_kernel(in_ref, factor_ref, out_ref, tile_ref):
    low = low_lanes(128)
    factor = factor_ref[0, 0]

    def piece(row):
        return in_ref[row].astype(F32)

    for tile in range(15):
        if tile < 7:
            value = jnp.where(low, piece(2 * tile), swap_halves(piece(2 * tile + 1)))
        elif tile == 7:
            value = jnp.where(low, piece(14) + swap_halves(piece(0)), piece(1))
        elif tile < 14:
            value = jnp.where(
                low, swap_halves(piece(2 * tile - 14)), piece(2 * tile - 13)
            )
        else:
            value = swap_halves(piece(14))
        tile_ref[...] = value * factor
        end = min(128 * tile + 128, WIDTH)
        for l in range(8):
            rows = tile_ref[pl.ds(l, 16, stride=8), :]
            out_ref[l, :, 128 * tile : end] = rows[:, : end - 128 * tile]


def vmem(count):
    return [pl.BlockSpec(memory_space=pltpu.VMEM) for _ in range(count)]


def call(kernel, out, in_specs, scratch=()):
    many = isinstance(out, tuple)
    return pl.pallas_call(
        kernel,
        out_shape=out,
        in_specs=in_specs,
        out_specs=tuple(vmem(len(out))) if many else vmem(1)[0],
        scratch_shapes=list(scratch),
        compiler_params=pltpu.CompilerParams(vmem_limit_bytes=VMEM_LIMIT),
    )


def shards(hidden_acts, output_errors, col_points, row_points, worker_mask):
    shape = jax.ShapeDtypeStruct
    half = (lax.axis_index("col_1") % 2).astype(jnp.int32).reshape(1)
    packed = call(
        pack_kernel,
        shape((N_ROW * N_Z, 16, 128), BF16),
        [pl.BlockSpec(memory_space=pltpu.SMEM)] + vmem(2),
        [pltpu.VMEM((16, 1024), F32)],
    )(half, hidden_acts, output_errors)
    packed = lax.all_to_all(packed, ROW_Z, 0, 0, tiled=True)
    mix = call(mix_kernel, shape((128, 128), F32), vmem(3))(
        col_points[None, :], row_points[None, :], worker_mask
    )
    spread = call(spread_kernel, shape((N_X, 1088, 128), BF16), vmem(1))(packed)
    spread = lax.all_to_all(spread, "col_0", 0, 0, tiled=True)
    mixed, squares = call(
        product_kernel,
        (shape((N_ROW, 128, 128), BF16), shape((8, 128), F32)),
        vmem(2),
        [pltpu.VMEM((2048, 128), F32)],
    )(spread, mix)
    squares = jnp.broadcast_to(jnp.sum(squares), (N_COL, 1, 128))
    squares = jnp.sum(lax.all_to_all(squares, COL, 0, 0, tiled=True)[:, 0, 0])
    squares = jnp.broadcast_to(squares, (N_ROW, 1, 128))
    squares = jnp.sum(lax.all_to_all(squares, ROW, 0, 0, tiled=True)[:, 0, 0])
    mixed = lax.all_to_all(mixed, ROW, 0, 0, tiled=True)
    factor = jnp.minimum(1.0, jnp.sqrt(jnp.float32(FF * D)) / jnp.sqrt(squares + 1e-06))
    return call(
        place_kernel,
        shape((8, 16, WIDTH), F32),
        vmem(1) + [pl.BlockSpec(memory_space=pltpu.SMEM)],
        [pltpu.VMEM((128, 128), F32)],
    )(mixed, factor.reshape(1, 1))


def solution(mesh):
    finer = Mesh(mesh.devices.reshape(8, 2, 4, 8), ROW + COL)
    in_specs = (P(ROW, COL), P(COL, ROW), P(), P(), P())
    return jax.shard_map(
        shards, mesh=finer, in_specs=in_specs, out_specs=P(None, COL, ROW), check_vma=False
    )
```

```python
import functools

import jax
import jax.numpy as jnp
from jax import lax
from jax.experimental import pallas as pl
from jax.experimental.pallas import tpu as pltpu
from jax.sharding import Mesh
from jax.sharding import PartitionSpec as P

D = 4096
FF = 29568
ROW = ("row_0", "row_1")
COL = ("col_0", "col_1")
ROW_Z = ("row_0", "row_1", "col_1")
N_ROW = 16
N_X = 4
N_Z = 8
N_COL = 32
HALF = FF // N_COL
WIDTH = FF // N_ROW
CHUNK = 64
SHIFT = HALF - (HALF // CHUNK) * CHUNK
BF16 = jnp.bfloat16
F32 = jnp.float32
VMEM_LIMIT = 48 * 1024 * 1024


def low_lanes(rows):
    return lax.broadcasted_iota(jnp.int32, (rows, 128), 1) < 64


def swap_halves(tile):
    return pltpu.roll(tile, 64, 1)


def pack_kernel(acts_ref, errs_ref, out_ref, padded, packed):
    padded[...] = jnp.zeros_like(padded)
    padded[:, :HALF] = acts_ref[...].astype(F32)
    plain = padded[...]
    second_half = lax.rem(lax.axis_index("col_1"), 2) == 1
    acts = jnp.where(second_half, pltpu.roll(plain, SHIFT, 1), plain)
    errs = errs_ref[...].astype(F32)
    low = low_lanes(8)
    lane = lax.broadcasted_iota(jnp.int32, (8, 128), 1)
    quarter = lane[:2] // 32
    err_tiles = []
    for z in range(N_Z):
        first = pltpu.roll(errs[:, :128], (128 - 16 * z) % 128, 1)
        second = pltpu.roll(errs[:, 128:], (144 - 16 * z) % 128, 1)
        both = jnp.where(lane < 16, first, second)
        tile = both[:2]
        for v in range(1, 4):
            turned = pltpu.roll(both, 32 * v, 1)
            tile = jnp.where(quarter == v, turned[2 * v : 2 * v + 2], tile)
        err_tiles.append(tile)
    for row in range(N_ROW):
        lanes = slice(128 * (row // 2), 128 * (row // 2) + 128)
        upper, lower = acts[:8, lanes], acts[8:, lanes]
        if row % 2 == 0:
            tile = jnp.where(low, upper, swap_halves(lower))
        else:
            tile = jnp.where(low, swap_halves(upper), lower)
        for z in range(N_Z):
            start = (row * N_Z + z) * 10
            packed[start : start + 8, :] = tile
            packed[start + 8 : start + 10, :] = err_tiles[z]
    out_ref[...] = packed[...].astype(BF16)


def spread_kernel(in_ref, out_ref, packed):
    packed[...] = in_ref[...].astype(F32)
    group = lax.broadcasted_iota(jnp.int32, (8, 128), 1) // 16
    for z in range(N_Z):
        starts = [(row * N_Z + z) * 10 for row in range(N_ROW)]
        acts = jnp.concatenate([packed[s : s + 8, :] for s in starts], axis=0)
        acts = acts.astype(BF16)
        for x in range(N_X):
            out_ref[x, 128 * z : 128 * z + 128, :] = acts
    for parity in range(2):
        sums = [[jnp.zeros((8, 128), F32) for _ in range(8)] for _ in range(2)]
        for block in range(8):
            for part in range(2):
                starts = [
                    ((2 * block + parity) * N_Z + z) * 10 + 8
                    for z in range(part, N_Z, 2)
                ]
                source = jnp.concatenate(
                    [packed[s : s + 2, :] for s in starts], axis=0
                )
                for v in range(4):
                    for q in range(2):
                        turned = pltpu.roll(
                            source, (128 + 16 * (block - q) - 32 * v) % 128, 1
                        )
                        place = 4 * part + v
                        sums[q][place] = jnp.where(
                            group == block, turned, sums[q][place]
                        )
        for q in range(2):
            errs = jnp.concatenate(sums[q], axis=0).astype(BF16)
            out_ref[2 * parity + q, 1024:1088, :] = errs


def node_value(index, count):
    return jnp.cos(jnp.pi * (2.0 * index.astype(F32) + 1.0) / (2.0 * count))


def parity_sign(count):
    return (1 - 2 * (count % 2)).astype(F32)


def mix_kernel(cols_ref, rows_ref, mask_ref, out_ref):
    iota = functools.partial(lax.broadcasted_iota, jnp.int32)
    cols = cols_ref[...]
    rows = rows_ref[...]
    live = mask_ref[...]
    col_eye = iota((N_COL, N_COL), 0) == iota((N_COL, N_COL), 1)
    row_eye = iota((N_ROW, N_ROW), 0) == iota((N_ROW, N_ROW), 1)
    col_point = jnp.sum(jnp.where(col_eye, cols, 0), axis=1, keepdims=True)
    row_point = jnp.sum(jnp.where(row_eye, rows, 0), axis=1, keepdims=True)
    work_acts = node_value(col_point, 2 * N_COL + 1)
    work_errs = node_value(row_point, 2 * N_ROW + 1)
    row_rank = jnp.sum((rows < row_point).astype(jnp.int32), axis=1, keepdims=True)
    row_sign = parity_sign(row_rank)

    lane = iota((1, 128), 1)
    err_in, act_in = lane // 16, lane % 16
    term = parity_sign(err_in) / (work_errs - node_value(err_in, 8))
    total = jnp.sum(jnp.where(act_in == 0, term, 0.0), axis=1, keepdims=True)
    encode_errs = term / total
    term = parity_sign(act_in) / (work_acts - node_value(act_in, 16))
    total = jnp.sum(jnp.where(err_in == 0, term, 0.0), axis=1, keepdims=True)
    encode_acts = term / total
    act_out, err_out = lane // 8, lane % 8
    term = row_sign / (node_value(err_out, 8) - work_errs)
    decode_errs = term / jnp.sum(term, axis=0, keepdims=True)
    inverse = 1.0 / (node_value(act_out, 16) - work_acts)

    lower = cols < col_point
    left, right = [], []
    for i in range(N_ROW):
        here = live[i : i + 1, :]
        rank = jnp.sum(jnp.where(lower, here, 0), axis=1, keepdims=True)
        own = jnp.sum(jnp.where(col_eye, here, 0), axis=1, keepdims=True)
        term = (own.astype(F32) * parity_sign(rank)) * inverse
        decode = term / jnp.sum(term, axis=0, keepdims=True)
        left.append(decode * decode_errs[i : i + 1, :])
        right.append(encode_acts * encode_errs[i : i + 1, :])
    total = lax.dot_general(
        jnp.concatenate(left, axis=0),
        jnp.concatenate(right, axis=0),
        (((0,), (0,)), ((), ())),
        preferred_element_type=F32,
        precision=lax.Precision.HIGHEST,
    )
    out_ref[...] = total.astype(BF16)


def product_kernel(in_ref, mix_ref, out_ref, squares_ref, products):
    low = low_lanes(128)
    errs = jnp.concatenate(
        [
            in_ref[x, 1024 + 32 * part : 1056 + 32 * part, :]
            for part in range(2)
            for x in range(N_X)
        ],
        axis=0,
    )
    here = lax.broadcasted_iota(jnp.int32, (256, 256), 0)
    there = lax.broadcasted_iota(jnp.int32, (256, 256), 1)
    source = there // 32 * 32 + there // 2 % 4 * 8 + there // 8 % 4 * 2 + there % 2
    errs = lax.dot_general(
        errs,
        jnp.where(here == source, 1.0, 0.0).astype(BF16),
        (((0,), (0,)), ((), ())),
        preferred_element_type=F32,
    ).astype(BF16)
    for block in range(16):
        x, z = block // 4, 2 * (block % 4)
        first = in_ref[x, 128 * z : 128 * z + 128, :].astype(F32)
        second = in_ref[x, 128 * z + 128 : 128 * z + 256, :].astype(F32)
        acts = jnp.concatenate(
            [
                jnp.where(low, first, swap_halves(second)),
                jnp.where(low, swap_halves(first), second),
            ],
            axis=0,
        ).astype(BF16)
        products[pl.ds(block, 128, stride=16), :] = jnp.dot(
            errs, acts, preferred_element_type=F32
        )
    mix = mix_ref[...]
    squares = jnp.zeros((128, 128), F32)
    for pair in range(8):
        mixed = []
        for r in (2 * pair, 2 * pair + 1):
            piece = jnp.concatenate(
                [
                    products[(block * 16 + r) * 16 : (block * 16 + r) * 16 + 16, :]
                    for block in range(8)
                ],
                axis=0,
            ).astype(BF16)
            grad = jnp.dot(mix, piece, preferred_element_type=F32)
            squares = squares + grad * grad
            mixed.append(grad)
        for k in range(N_ROW):
            both = jnp.concatenate(
                [grad[8 * k : 8 * k + 8, :] for grad in mixed], axis=0
            )
            out_ref[k, 16 * pair : 16 * pair + 16, :] = both.astype(BF16)
    squares_ref[...] = jnp.full(squares_ref.shape, jnp.sum(squares), F32)


def carry_kernel(in_ref, squares_ref, out_ref):
    out_ref[:, :128, :] = in_ref[...]
    total = jnp.sum(squares_ref[...], axis=0)
    high = total.astype(BF16).astype(F32)
    middle = (total - high).astype(BF16).astype(F32)
    row = lax.broadcasted_iota(jnp.int32, (8, 128), 0)
    rows = jnp.where(row == 0, high, jnp.where(row == 1, middle, total - high - middle))
    rows = jnp.where(row < 3, rows, 0.0).astype(BF16)
    for k in range(N_ROW):
        out_ref[k, 128:136, :] = rows


def place_kernel(in_ref, out_ref, tile_ref):
    low = low_lanes(128)
    squares = jnp.zeros((8, 128), F32)
    for row in range(N_ROW):
        squares = squares + in_ref[row, 128:136, :].astype(F32)
    squares = jnp.sum(squares, axis=0, keepdims=True)
    factor = jnp.minimum(1.0, jnp.sqrt(jnp.float32(FF * D)) / jnp.sqrt(squares + 1e-06))

    def piece(row):
        return in_ref[row, :128, :].astype(F32)

    for tile in range(15):
        if tile < 7:
            value = jnp.where(low, piece(2 * tile), swap_halves(piece(2 * tile + 1)))
        elif tile == 7:
            value = jnp.where(low, piece(14) + swap_halves(piece(0)), piece(1))
        elif tile < 14:
            value = jnp.where(
                low, swap_halves(piece(2 * tile - 14)), piece(2 * tile - 13)
            )
        else:
            value = swap_halves(piece(14))
        tile_ref[...] = value * factor
        end = min(128 * tile + 128, WIDTH)
        for l in range(8):
            rows = tile_ref[pl.ds(l, 16, stride=8), :]
            out_ref[l, :, 128 * tile : end] = rows[:, : end - 128 * tile]


def vmem(count):
    return [pl.BlockSpec(memory_space=pltpu.VMEM) for _ in range(count)]


def call(kernel, out, in_specs, scratch=()):
    many = isinstance(out, tuple)
    return pl.pallas_call(
        kernel,
        out_shape=out,
        in_specs=in_specs,
        out_specs=tuple(vmem(len(out))) if many else vmem(1)[0],
        scratch_shapes=list(scratch),
        compiler_params=pltpu.CompilerParams(vmem_limit_bytes=VMEM_LIMIT),
    )


def shards(hidden_acts, output_errors, col_points, row_points, worker_mask):
    shape = jax.ShapeDtypeStruct
    packed = call(
        pack_kernel,
        shape((N_ROW * N_Z * 10, 128), BF16),
        vmem(2),
        [
            pltpu.VMEM((16, 1024), F32),
            pltpu.VMEM((N_ROW * N_Z * 10, 128), F32),
        ],
    )(hidden_acts, output_errors)
    mix = call(mix_kernel, shape((128, 128), BF16), vmem(3))(
        col_points[None, :], row_points[None, :], worker_mask
    )
    packed = packed.reshape(N_ROW * N_Z, 5, 2, 128)
    packed = lax.all_to_all(packed, ROW_Z, 0, 0, tiled=True)
    spread = call(
        spread_kernel,
        shape((N_X, 1088, 128), BF16),
        vmem(1),
        [pltpu.VMEM((N_ROW * N_Z * 10, 128), F32)],
    )(packed.reshape(N_ROW * N_Z * 10, 128))
    spread = lax.all_to_all(spread, "col_0", 0, 0, tiled=True)
    mixed, squares = call(
        product_kernel,
        (shape((N_ROW, 128, 128), BF16), shape((N_COL, 1, 128), F32)),
        vmem(2),
        [pltpu.VMEM((2048, 128), F32)],
    )(spread, mix)
    squares = lax.all_to_all(squares, COL, 0, 0, tiled=True)
    mixed = call(carry_kernel, shape((N_ROW, 136, 128), BF16), vmem(2))(mixed, squares)
    mixed = lax.all_to_all(mixed, ROW, 0, 0, tiled=True)
    return call(
        place_kernel,
        shape((8, 16, WIDTH), F32),
        vmem(1),
        [pltpu.VMEM((128, 128), F32)],
    )(mixed)


def solution(mesh):
    finer = Mesh(mesh.devices.reshape(8, 2, 4, 8), ROW + COL)
    in_specs = (P(ROW, COL), P(COL, ROW), P(), P(), P())
    return jax.shard_map(
        shards, mesh=finer, in_specs=in_specs, out_specs=P(None, COL, ROW), check_vma=False
    )
```

```python
import functools

import jax
import jax.numpy as jnp
from jax import lax
from jax.experimental import pallas as pl
from jax.experimental.pallas import tpu as pltpu
from jax.sharding import Mesh
from jax.sharding import PartitionSpec as P

D = 4096
FF = 29568
ROW = ("row_0", "row_1")
COL = ("col_0", "col_1")
ROW_X = ("row_0", "row_1", "col_0")
ROW_Z = ("row_0", "row_1", "col_1")
N_ROW = 16
N_X = 4
N_Z = 8
N_COL = 32
HALF = FF // N_COL
WIDTH = FF // N_ROW
CHUNK = 64
SHIFT = HALF - (HALF // CHUNK) * CHUNK
BF16 = jnp.bfloat16
F32 = jnp.float32
VMEM_LIMIT = 48 * 1024 * 1024


def low_lanes(rows):
    return lax.broadcasted_iota(jnp.int32, (rows, 128), 1) < 64


def swap_halves(tile):
    return pltpu.roll(tile, 64, 1)


def pack_kernel(acts_ref, errs_ref, out_ref, padded, packed):
    padded[...] = jnp.zeros_like(padded)
    padded[:, :HALF] = acts_ref[...].astype(F32)
    plain = padded[...]
    second_half = lax.rem(lax.axis_index("col_1"), 2) == 1
    acts = jnp.where(second_half, pltpu.roll(plain, SHIFT, 1), plain)
    errs = errs_ref[...].astype(F32)
    low = low_lanes(8)
    up = 32 * lax.div(lax.axis_index("col_1"), 2)
    lane = lax.broadcasted_iota(jnp.int32, (8, 128), 1)
    quarter = lane[:2] // 32
    err_tiles = []
    for z in range(N_Z):
        first = pltpu.roll(errs[:, :128], (128 - 16 * z) % 128, 1)
        second = pltpu.roll(errs[:, 128:], (144 - 16 * z) % 128, 1)
        both = jnp.where(lane < 16, first, second)
        tile = both[:2]
        for v in range(1, 4):
            turned = pltpu.roll(both, 32 * v, 1)
            tile = jnp.where(quarter == v, turned[2 * v : 2 * v + 2], tile)
        err_tiles.append(tile)
    for row in range(N_ROW):
        lanes = slice(128 * (row // 2), 128 * (row // 2) + 128)
        upper, lower = acts[:8, lanes], acts[8:, lanes]
        if row % 2 == 0:
            tile = jnp.where(low, upper, swap_halves(lower))
        else:
            tile = jnp.where(low, swap_halves(upper), lower)
        tile = pltpu.roll(tile, up, 1)
        for z in range(N_Z):
            start = (row * N_Z + z) * 10
            packed[start : start + 8, :] = tile
            packed[start + 8 : start + 10, :] = err_tiles[z]
    out_ref[...] = packed[...].astype(BF16)


def gather_group(tiles, which):
    rows = tiles[0].shape[0]
    wanted = lax.broadcasted_iota(jnp.int32, (rows, 128), 1) // 32
    result = tiles[-which % 4]
    for place in range(1, 4):
        result = jnp.where(wanted == place, tiles[(place - which) % 4], result)
    return pltpu.roll(result, 128 - 32 * which, 1) if which else result


def spread_kernel(in_ref, out_ref, packed):
    packed[...] = in_ref[...].astype(F32)
    group = lax.broadcasted_iota(jnp.int32, (8, 128), 1) // 16
    for pair in range(N_ROW // 2):
        for half in range(2):
            sources = []
            for row in (2 * pair, 2 * pair + 1):
                starts = [(row * N_Z + z) * 10 for z in range(half, N_Z, 2)]
                sources.append([packed[s : s + 8, :] for s in starts])
            for part in range(2):
                for q in range(2):
                    both = jnp.concatenate(
                        [gather_group(tiles, 2 * part + q) for tiles in sources], axis=0
                    )
                    start = 128 * part + 16 * pair
                    out_ref[2 * half + q, start : start + 16, :] = both.astype(BF16)
    for parity in range(2):
        sums = [[jnp.zeros((8, 128), F32) for _ in range(8)] for _ in range(2)]
        for block in range(8):
            for part in range(2):
                starts = [
                    ((2 * block + parity) * N_Z + z) * 10 + 8
                    for z in range(part, N_Z, 2)
                ]
                source = jnp.concatenate(
                    [packed[s : s + 2, :] for s in starts], axis=0
                )
                for v in range(4):
                    for q in range(2):
                        turned = pltpu.roll(
                            source, (128 + 16 * (block - q) - 32 * v) % 128, 1
                        )
                        place = 4 * part + v
                        sums[q][place] = jnp.where(
                            group == block, turned, sums[q][place]
                        )
        for q in range(2):
            errs = jnp.concatenate(sums[q], axis=0).astype(BF16)
            start = 256 + 64 * (2 * parity + q)
            for x in range(N_X):
                out_ref[x, start : start + 64, :] = errs


def node_value(index, count):
    return jnp.cos(jnp.pi * (2.0 * index.astype(F32) + 1.0) / (2.0 * count))


def parity_sign(count):
    return (1 - 2 * (count % 2)).astype(F32)


def mix_kernel(cols_ref, rows_ref, mask_ref, out_ref):
    iota = functools.partial(lax.broadcasted_iota, jnp.int32)
    cols = cols_ref[...]
    rows = rows_ref[...]
    live = mask_ref[...]
    col_eye = iota((N_COL, N_COL), 0) == iota((N_COL, N_COL), 1)
    row_eye = iota((N_ROW, N_ROW), 0) == iota((N_ROW, N_ROW), 1)
    col_point = jnp.sum(jnp.where(col_eye, cols, 0), axis=1, keepdims=True)
    row_point = jnp.sum(jnp.where(row_eye, rows, 0), axis=1, keepdims=True)
    work_acts = node_value(col_point, 2 * N_COL + 1)
    work_errs = node_value(row_point, 2 * N_ROW + 1)
    row_rank = jnp.sum((rows < row_point).astype(jnp.int32), axis=1, keepdims=True)
    row_sign = parity_sign(row_rank)

    lane = iota((1, 128), 1)
    err_in, act_in = lane // 16, lane % 16
    term = parity_sign(err_in) / (work_errs - node_value(err_in, 8))
    total = jnp.sum(jnp.where(act_in == 0, term, 0.0), axis=1, keepdims=True)
    encode_errs = term / total
    term = parity_sign(act_in) / (work_acts - node_value(act_in, 16))
    total = jnp.sum(jnp.where(err_in == 0, term, 0.0), axis=1, keepdims=True)
    encode_acts = term / total
    act_out, err_out = lane // 8, lane % 8
    term = row_sign / (node_value(err_out, 8) - work_errs)
    decode_errs = term / jnp.sum(term, axis=0, keepdims=True)
    inverse = 1.0 / (node_value(act_out, 16) - work_acts)

    lower = cols < col_point
    left, right = [], []
    for i in range(N_ROW):
        here = live[i : i + 1, :]
        rank = jnp.sum(jnp.where(lower, here, 0), axis=1, keepdims=True)
        own = jnp.sum(jnp.where(col_eye, here, 0), axis=1, keepdims=True)
        term = (own.astype(F32) * parity_sign(rank)) * inverse
        decode = term / jnp.sum(term, axis=0, keepdims=True)
        left.append(decode * decode_errs[i : i + 1, :])
        right.append(encode_acts * encode_errs[i : i + 1, :])
    total = lax.dot_general(
        jnp.concatenate(left, axis=0),
        jnp.concatenate(right, axis=0),
        (((0,), (0,)), ((), ())),
        preferred_element_type=F32,
        precision=lax.Precision.HIGHEST,
    )
    out_ref[...] = total.astype(BF16)


def one_hot(source, size):
    here = lax.broadcasted_iota(jnp.int32, (size, size), 0)
    return jnp.where(here == source, 1.0, 0.0).astype(BF16)


def product_kernel(in_ref, mix_ref, out_ref, squares_ref, products):
    to = lax.broadcasted_iota(jnp.int32, (256, 256), 1)
    tokens = one_hot(
        to // 32 * 32 + to // 2 % 4 * 8 + to // 8 % 4 * 2 + to % 2, 256
    )
    to = lax.broadcasted_iota(jnp.int32, (128, 128), 1)
    up = 2 * lax.axis_index("row_1") + lax.rem(lax.axis_index("col_0"), 2)
    features = one_hot(to % 8 * 16 + to // 8 % 4 * 4 + (to // 32 + 4 - up) % 4, 128)
    turned = []
    for target in range(N_X):
        errs = jnp.concatenate(
            [
                in_ref[x, start : start + 32, :]
                for start in (256 + 64 * target, 288 + 64 * target)
                for x in range(N_X)
            ],
            axis=0,
        )
        errs = jnp.dot(errs, features, preferred_element_type=F32).astype(BF16)
        turned.append(
            lax.dot_general(
                errs, tokens, (((0,), (0,)), ((), ())), preferred_element_type=F32
            ).astype(BF16)
        )
    errs = jnp.concatenate(
        [tile[32 * r : 32 * r + 32, :] for r in range(4) for tile in turned], axis=0
    )
    for x in range(N_X):
        product = jnp.dot(errs, in_ref[x, :256, :], preferred_element_type=F32)
        tiles = [product[128 * r : 128 * r + 128, :] for r in range(4)]
        tiles = [pltpu.roll(tile, 32 * r, 1) if r else tile for r, tile in enumerate(tiles)]
        for i in range(4):
            products[pl.ds(4 * x + i, 128, stride=16), :] = gather_group(tiles, i)
    mix = mix_ref[...]
    squares = jnp.zeros((128, 128), F32)
    for pair in range(8):
        mixed = []
        for s in (2 * pair, 2 * pair + 1):
            piece = products[128 * s : 128 * s + 128, :].astype(BF16)
            grad = jnp.dot(mix, piece, preferred_element_type=F32)
            squares = squares + grad * grad
            mixed.append(grad)
        start = 16 * (pair % 2)
        for k in range(N_ROW):
            both = jnp.concatenate(
                [grad[8 * k : 8 * k + 8, :] for grad in mixed], axis=0
            )
            out_ref[N_X * k + pair // 2, start : start + 16, :] = both.astype(BF16)
    squares_ref[...] = jnp.full(squares_ref.shape, jnp.sum(squares), F32)


def carry_kernel(in_ref, squares_ref, out_ref, packed):
    total = jnp.sum(squares_ref[...], axis=0)
    high = total.astype(BF16).astype(F32)
    middle = (total - high).astype(BF16).astype(F32)
    last = total - high - middle
    row = lax.broadcasted_iota(jnp.int32, (2, 128), 0)
    lane = lax.broadcasted_iota(jnp.int32, (2, 128), 1)
    rows = jnp.where(row == 0, high, jnp.where(lane < 64, middle, last))
    for peer in range(N_ROW * N_X):
        packed[34 * peer : 34 * peer + 32, :] = in_ref[peer].astype(F32)
        packed[34 * peer + 32 : 34 * peer + 34, :] = rows
    out_ref[...] = packed[...].astype(BF16)


def place_kernel(in_ref, out_ref, packed, tile_ref):
    packed[...] = in_ref[...].astype(F32)
    squares = jnp.zeros((2, 128), F32)
    for peer in range(N_ROW * N_X):
        squares = squares + packed[34 * peer + 32 : 34 * peer + 34, :]
    squares = squares[:1, :1] + squares[1:, :1] + squares[1:, 64:65]
    factor = jnp.minimum(1.0, jnp.sqrt(jnp.float32(FF * D)) / jnp.sqrt(squares + 1e-06))

    for s in range(4):
        for j in range(8):
            for half in range(2):
                peers = [8 * j + 4 * a + 2 * half + q for a in range(2) for q in range(2)]
                starts = [34 * peer + 8 * s for peer in peers]
                tiles = [packed[start : start + 8, :] * factor for start in starts]
                for r in range(4):
                    start = (4 * s + r) * 8
                    value = gather_group(tiles, r)
                    if half == 0 and j == 7:
                        value = value + tile_ref[7, start : start + 8, :]
                    tile_ref[j + 7 * half, start : start + 8, :] = value
    for tile in range(15):
        end = min(128 * tile + 128, WIDTH)
        for l in range(8):
            rows = tile_ref[tile, pl.ds(l, 16, stride=8), :]
            out_ref[l, :, 128 * tile : end] = rows[:, : end - 128 * tile]


def vmem(count):
    return [pl.BlockSpec(memory_space=pltpu.VMEM) for _ in range(count)]


def call(kernel, out, in_specs, scratch=()):
    many = isinstance(out, tuple)
    return pl.pallas_call(
        kernel,
        out_shape=out,
        in_specs=in_specs,
        out_specs=tuple(vmem(len(out))) if many else vmem(1)[0],
        scratch_shapes=list(scratch),
        compiler_params=pltpu.CompilerParams(vmem_limit_bytes=VMEM_LIMIT),
    )


def shards(hidden_acts, output_errors, col_points, row_points, worker_mask):
    shape = jax.ShapeDtypeStruct
    packed = call(
        pack_kernel,
        shape((N_ROW * N_Z * 10, 128), BF16),
        vmem(2),
        [
            pltpu.VMEM((16, 1024), F32),
            pltpu.VMEM((N_ROW * N_Z * 10, 128), F32),
        ],
    )(hidden_acts, output_errors)
    mix = call(mix_kernel, shape((128, 128), BF16), vmem(3))(
        col_points[None, :], row_points[None, :], worker_mask
    )
    packed = packed.reshape(N_ROW * N_Z, 5, 2, 128)
    packed = lax.all_to_all(packed, ROW_Z, 0, 0, tiled=True)
    spread = call(
        spread_kernel,
        shape((N_X, 512, 128), BF16),
        vmem(1),
        [pltpu.VMEM((N_ROW * N_Z * 10, 128), F32)],
    )(packed.reshape(N_ROW * N_Z * 10, 128))
    spread = lax.all_to_all(spread, "col_0", 0, 0, tiled=True)
    peers = N_ROW * N_X
    mixed, squares = call(
        product_kernel,
        (shape((peers, 32, 128), BF16), shape((N_Z, 1, 128), F32)),
        vmem(2),
        [pltpu.VMEM((2048, 128), F32)],
    )(spread, mix)
    squares = lax.all_to_all(squares, "col_1", 0, 0, tiled=True)
    mixed = call(
        carry_kernel,
        shape((peers * 34, 128), BF16),
        vmem(2),
        [pltpu.VMEM((peers * 34, 128), F32)],
    )(mixed, squares)
    mixed = lax.all_to_all(mixed.reshape(peers, 17, 2, 128), ROW_X, 0, 0, tiled=True)
    return call(
        place_kernel,
        shape((8, 16, WIDTH), F32),
        vmem(1),
        [pltpu.VMEM((peers * 34, 128), F32), pltpu.VMEM((15, 128, 128), F32)],
    )(mixed.reshape(peers * 34, 128))


def solution(mesh):
    finer = Mesh(mesh.devices.reshape(8, 2, 4, 8), ROW + COL)
    in_specs = (P(ROW, COL), P(COL, ROW), P(), P(), P())
    return jax.shard_map(
        shards, mesh=finer, in_specs=in_specs, out_specs=P(None, COL, ROW), check_vma=False
    )
```

```python
import functools

import jax
import jax.numpy as jnp
from jax import lax
from jax.experimental import pallas as pl
from jax.experimental.pallas import tpu as pltpu
from jax.sharding import Mesh
from jax.sharding import PartitionSpec as P

D = 4096
FF = 29568
ROW = ("row_0", "row_1")
COL = ("col_0", "col_1")
X_ROW = ("col_0", "row_1", "row_0")
Z_ROW = ("col_1", "row_1", "row_0")
N_ROW = 16
N_X = 4
N_Z = 8
N_COL = 32
HALF = FF // N_COL
WIDTH = FF // N_ROW
CHUNK = 64
SHIFT = HALF - (HALF // CHUNK) * CHUNK
BF16 = jnp.bfloat16
F32 = jnp.float32
VMEM_LIMIT = 48 * 1024 * 1024


def place_among(other, row):
    return (other * 2 + row % 2) * (N_ROW // 2) + row // 2


def low_lanes(rows):
    return lax.broadcasted_iota(jnp.int32, (rows, 128), 1) < 64


def swap_halves(tile):
    return pltpu.roll(tile, 64, 1)


def pack_kernel(
    acts_in, errs_in, cols_in, rows_in, mask_in,
    out_ref, cols_ref, rows_ref, mask_ref,
    acts_ref, errs_ref, padded, packed, sems,
):
    pairs = (
        (acts_in, acts_ref),
        (errs_in, errs_ref),
        (cols_in, cols_ref),
        (rows_in, rows_ref),
        (mask_in, mask_ref),
    )
    copies = [
        pltpu.make_async_copy(source, target, sems.at[i])
        for i, (source, target) in enumerate(pairs)
    ]
    for copy in copies:
        copy.start()
    for copy in copies:
        copy.wait()
    padded[...] = jnp.zeros_like(padded)
    padded[:, :HALF] = acts_ref[...].astype(F32)
    plain = padded[...]
    second_half = lax.rem(lax.axis_index("col_1"), 2) == 1
    acts = jnp.where(second_half, pltpu.roll(plain, SHIFT, 1), plain)
    errs = errs_ref[...].astype(F32)
    low = low_lanes(8)
    up = 32 * lax.div(lax.axis_index("col_1"), 2)
    lane = lax.broadcasted_iota(jnp.int32, (8, 128), 1)
    quarter = lane[:2] // 32
    err_tiles = []
    for z in range(N_Z):
        first = pltpu.roll(errs[:, :128], (128 - 16 * z) % 128, 1)
        second = pltpu.roll(errs[:, 128:], (144 - 16 * z) % 128, 1)
        both = jnp.where(lane < 16, first, second)
        tile = both[:2]
        for v in range(1, 4):
            turned = pltpu.roll(both, 32 * v, 1)
            tile = jnp.where(quarter == v, turned[2 * v : 2 * v + 2], tile)
        err_tiles.append(pltpu.roll(tile, 16 * lax.axis_index("row_0"), 1))
    for row in range(N_ROW):
        lanes = slice(128 * (row // 2), 128 * (row // 2) + 128)
        upper, lower = acts[:8, lanes], acts[8:, lanes]
        if row % 2 == 0:
            tile = jnp.where(low, upper, swap_halves(lower))
        else:
            tile = jnp.where(low, swap_halves(upper), lower)
        tile = pltpu.roll(tile, up, 1)
        for z in range(N_Z):
            start = place_among(z, row) * 10
            packed[start : start + 8, :] = tile
            packed[start + 8 : start + 10, :] = err_tiles[z]
    out_ref[...] = packed[: out_ref.shape[0], :].astype(BF16)


def gather_group(tiles, which):
    count = len(tiles)
    width = 128 // count
    rows = tiles[0].shape[0]
    wanted = lax.broadcasted_iota(jnp.int32, (rows, 128), 1) // width
    result = tiles[-which % count]
    for place in range(1, count):
        result = jnp.where(wanted == place, tiles[(place - which) % count], result)
    return pltpu.roll(result, 128 - width * which, 1) if which else result


def spread_kernel(in_ref, out_ref, packed):
    packed[: in_ref.shape[0], :] = in_ref[...].astype(F32)
    for pair in range(N_ROW // 2):
        for half in range(2):
            sources = []
            for row in (2 * pair, 2 * pair + 1):
                starts = [place_among(z, row) * 10 for z in range(half, N_Z, 2)]
                sources.append([packed[s : s + 8, :] for s in starts])
            for part in range(2):
                for q in range(2):
                    both = jnp.concatenate(
                        [gather_group(tiles, 2 * part + q) for tiles in sources], axis=0
                    )
                    start = 128 * part + 16 * pair
                    out_ref[2 * half + q, start : start + 16, :] = both.astype(BF16)
    for parity in range(2):
        pieces = [[], []]
        for part in range(2):
            sources = []
            for block in range(8):
                starts = [
                    place_among(z, 2 * block + parity) * 10 + 8
                    for z in range(part, N_Z, 2)
                ]
                sources.append(
                    jnp.concatenate([packed[s : s + 2, :] for s in starts], axis=0)
                )
            for v in range(4):
                for q in range(2):
                    pieces[q].append(gather_group(sources, 2 * v + q))
        for q in range(2):
            errs = jnp.concatenate(pieces[q], axis=0).astype(BF16)
            start = 256 + 64 * (2 * parity + q)
            for x in range(N_X):
                out_ref[x, start : start + 64, :] = errs


def node_value(index, count):
    return jnp.cos(jnp.pi * (2.0 * index.astype(F32) + 1.0) / (2.0 * count))


def parity_sign(count):
    return (1 - 2 * (count % 2)).astype(F32)


def mix_matrix(cols_ref, rows_ref, mask_ref):
    iota = functools.partial(lax.broadcasted_iota, jnp.int32)
    cols = cols_ref[...]
    rows = rows_ref[...]
    live = mask_ref[...]
    col_eye = iota((N_COL, N_COL), 0) == iota((N_COL, N_COL), 1)
    row_eye = iota((N_ROW, N_ROW), 0) == iota((N_ROW, N_ROW), 1)
    col_point = jnp.sum(jnp.where(col_eye, cols, 0), axis=1, keepdims=True)
    row_point = jnp.sum(jnp.where(row_eye, rows, 0), axis=1, keepdims=True)
    work_acts = node_value(col_point, 2 * N_COL + 1)
    work_errs = node_value(row_point, 2 * N_ROW + 1)
    row_rank = jnp.sum((rows < row_point).astype(jnp.int32), axis=1, keepdims=True)
    row_sign = parity_sign(row_rank)

    lane = iota((1, 128), 1)
    err_in, act_in = lane // 16, lane % 16
    term = parity_sign(err_in) / (work_errs - node_value(err_in, 8))
    total = jnp.sum(jnp.where(act_in == 0, term, 0.0), axis=1, keepdims=True)
    encode_errs = term / total
    term = parity_sign(act_in) / (work_acts - node_value(act_in, 16))
    total = jnp.sum(jnp.where(err_in == 0, term, 0.0), axis=1, keepdims=True)
    encode_acts = term / total
    act_out, err_out = lane // 8, lane % 8
    term = row_sign / (node_value(err_out, 8) - work_errs)
    decode_errs = term / jnp.sum(term, axis=0, keepdims=True)
    inverse = 1.0 / (node_value(act_out, 16) - work_acts)

    lower = cols < col_point
    left, right = [], []
    for i in range(N_ROW):
        here = live[i : i + 1, :]
        rank = jnp.sum(jnp.where(lower, here, 0), axis=1, keepdims=True)
        own = jnp.sum(jnp.where(col_eye, here, 0), axis=1, keepdims=True)
        term = (own.astype(F32) * parity_sign(rank)) * inverse
        decode = term / jnp.sum(term, axis=0, keepdims=True)
        left.append(decode * decode_errs[i : i + 1, :])
        right.append(encode_acts * encode_errs[i : i + 1, :])
    return lax.dot_general(
        jnp.concatenate(left, axis=0),
        jnp.concatenate(right, axis=0),
        (((0,), (0,)), ((), ())),
        preferred_element_type=F32,
        precision=lax.Precision.HIGHEST,
    ).astype(BF16)


def one_hot(source, size):
    here = lax.broadcasted_iota(jnp.int32, (size, size), 0)
    return jnp.where(here == source, 1.0, 0.0).astype(BF16)


def product_kernel(
    in_ref, cols_ref, rows_ref, mask_ref, out_ref, squares_ref, products
):
    mix = mix_matrix(cols_ref, rows_ref, mask_ref)
    to = lax.broadcasted_iota(jnp.int32, (256, 256), 1)
    tokens = one_hot(
        to // 32 * 32 + to // 2 % 4 * 8 + to // 8 % 4 * 2 + to % 2, 256
    )
    to = lax.broadcasted_iota(jnp.int32, (128, 128), 1)
    up = 2 * lax.axis_index("row_1") + lax.rem(lax.axis_index("col_0"), 2)
    features = one_hot(to % 8 * 16 + to // 8 % 4 * 4 + (to // 32 + 4 - up) % 4, 128)
    turned = []
    for target in range(N_X):
        errs = jnp.concatenate(
            [
                in_ref[x, start : start + 32, :]
                for start in (256 + 64 * target, 288 + 64 * target)
                for x in range(N_X)
            ],
            axis=0,
        )
        errs = jnp.dot(errs, features, preferred_element_type=F32).astype(BF16)
        turned.append(
            lax.dot_general(
                errs, tokens, (((0,), (0,)), ((), ())), preferred_element_type=F32
            ).astype(BF16)
        )
    errs = jnp.concatenate(
        [tile[32 * r : 32 * r + 32, :] for r in range(4) for tile in turned], axis=0
    )
    for x in range(0, N_X, 2):
        acts = jnp.concatenate([in_ref[x, :256, :], in_ref[x + 1, :256, :]], axis=1)
        product = jnp.dot(errs, acts, preferred_element_type=F32)
        for i in range(2):
            tiles = []
            for r in range(4):
                tile = product[128 * r : 128 * r + 128, 128 * i : 128 * i + 128]
                tiles.append(pltpu.roll(tile, 32 * r, 1) if r else tile)
            for z in range(4):
                where = pl.ds(4 * (x + i) + z, 128, stride=16)
                products[where, :] = gather_group(tiles, z)
    squares = jnp.zeros((128, 256), F32)
    for pair in range(8):
        both = [
            products[128 * s : 128 * s + 128, :].astype(BF16)
            for s in (2 * pair, 2 * pair + 1)
        ]
        grad = jnp.dot(mix, jnp.concatenate(both, axis=1), preferred_element_type=F32)
        squares = squares + grad * grad
        mixed = [grad[:, :128], grad[:, 128:]]
        start = 16 * (pair % 2)
        for k in range(N_ROW):
            both = jnp.concatenate(
                [grad[8 * k : 8 * k + 8, :] for grad in mixed], axis=0
            )
            out_ref[place_among(pair // 2, k), start : start + 16, :] = both.astype(BF16)
    squares_ref[...] = jnp.full(squares_ref.shape, jnp.sum(squares), F32)


def carry_kernel(in_ref, squares_ref, out_ref, packed):
    total = jnp.sum(squares_ref[...], axis=0)
    high = total.astype(BF16).astype(F32)
    middle = (total - high).astype(BF16).astype(F32)
    last = total - high - middle
    row = lax.broadcasted_iota(jnp.int32, (2, 128), 0)
    lane = lax.broadcasted_iota(jnp.int32, (2, 128), 1)
    rows = jnp.where(row == 0, high, jnp.where(lane < 64, middle, last))
    for peer in range(N_ROW * N_X):
        packed[34 * peer : 34 * peer + 32, :] = in_ref[peer].astype(F32)
        packed[34 * peer + 32 : 34 * peer + 34, :] = rows
    out_ref[...] = packed[: out_ref.shape[0], :].astype(BF16)


def place_kernel(in_ref, out_ref, packed, tile_ref):
    packed[: in_ref.shape[0], :] = in_ref[...].astype(F32)
    squares = jnp.zeros((2, 128), F32)
    for peer in range(N_ROW * N_X):
        squares = squares + packed[34 * peer + 32 : 34 * peer + 34, :]
    squares = squares[:1, :1] + squares[1:, :1] + squares[1:, 64:65]
    factor = jnp.minimum(1.0, jnp.sqrt(jnp.float32(FF * D)) / jnp.sqrt(squares + 1e-06))

    for s in range(4):
        for j in range(8):
            for half in range(2):
                peers = [
                    place_among(2 * half + q, 2 * j + a) for a in range(2) for q in range(2)
                ]
                starts = [34 * peer + 8 * s for peer in peers]
                tiles = [packed[start : start + 8, :] * factor for start in starts]
                for r in range(4):
                    start = (4 * s + r) * 8
                    value = gather_group(tiles, r)
                    if half == 0 and j == 7:
                        value = value + tile_ref[7, start : start + 8, :]
                    tile_ref[j + 7 * half, start : start + 8, :] = value
    for tile in range(15):
        end = min(128 * tile + 128, WIDTH)
        for l in range(8):
            rows = tile_ref[tile, pl.ds(l, 16, stride=8), :]
            out_ref[l, :, 128 * tile : end] = rows[:, : end - 128 * tile]


def vmem(count):
    return [pl.BlockSpec(memory_space=pltpu.VMEM) for _ in range(count)]


def call(kernel, out, in_specs, scratch=()):
    many = isinstance(out, tuple)
    return pl.pallas_call(
        kernel,
        out_shape=out,
        in_specs=in_specs,
        out_specs=tuple(vmem(len(out))) if many else vmem(1)[0],
        scratch_shapes=list(scratch),
        compiler_params=pltpu.CompilerParams(vmem_limit_bytes=VMEM_LIMIT),
    )


def shards(hidden_acts, output_errors, col_points, row_points, worker_mask):
    shape = jax.ShapeDtypeStruct
    args = (
        hidden_acts,
        output_errors,
        col_points[None, :],
        row_points[None, :],
        worker_mask,
    )
    points = tuple(shape(arg.shape, arg.dtype) for arg in args[2:])
    packed, *points = call(
        pack_kernel,
        (shape((N_ROW * N_Z * 10, 128), BF16), *points),
        [pl.BlockSpec(memory_space=pltpu.HBM)] * 5,
        [
            pltpu.VMEM((16, HALF), BF16),
            pltpu.VMEM((8, 256), BF16),
            pltpu.VMEM((16, 1024), F32),
            pltpu.VMEM((N_ROW * N_Z * 10 + 8, 128), F32),
            pltpu.SemaphoreType.DMA((5,)),
        ],
    )(*[pltpu.with_memory_space_constraint(arg, pltpu.HBM) for arg in args])
    packed = packed.reshape(N_ROW * N_Z, 5, 2, 128)
    packed = lax.all_to_all(packed, Z_ROW, 0, 0, tiled=True)
    spread = call(
        spread_kernel,
        shape((N_X, 512, 128), BF16),
        vmem(1),
        [pltpu.VMEM((N_ROW * N_Z * 10 + 8, 128), F32)],
    )(packed.reshape(N_ROW * N_Z * 10, 128))
    spread = lax.all_to_all(spread, "col_0", 0, 0, tiled=True)
    peers = N_ROW * N_X
    mixed, squares = call(
        product_kernel,
        (shape((peers, 32, 128), BF16), shape((N_Z, 1, 128), F32)),
        vmem(4),
        [pltpu.VMEM((2048 + 16, 128), F32)],
    )(spread, *points)
    squares = lax.all_to_all(squares, "col_1", 0, 0, tiled=True)
    mixed = call(
        carry_kernel,
        shape((peers * 34, 128), BF16),
        vmem(2),
        [pltpu.VMEM((peers * 34 + 8, 128), F32)],
    )(mixed, squares)
    mixed = lax.all_to_all(mixed.reshape(peers, 17, 2, 128), X_ROW, 0, 0, tiled=True)
    return call(
        place_kernel,
        shape((8, 16, WIDTH), F32),
        vmem(1),
        [pltpu.VMEM((peers * 34 + 8, 128), F32), pltpu.VMEM((15, 128 + 8, 128), F32)],
    )(mixed.reshape(peers * 34, 128))


def solution(mesh):
    finer = Mesh(mesh.devices.reshape(8, 2, 4, 8), ROW + COL)
    in_specs = (P(ROW, COL), P(COL, ROW), P(), P(), P())
    return jax.shard_map(
        shards, mesh=finer, in_specs=in_specs, out_specs=P(None, COL, ROW), check_vma=False
    )
```

```python
import functools

import jax
import jax.numpy as jnp
from jax import lax
from jax.experimental import pallas as pl
from jax.experimental.pallas import tpu as pltpu
from jax.sharding import Mesh
from jax.sharding import PartitionSpec as P

D = 4096
FF = 29568
ROW = ("row_0", "row_1")
COL = ("col_0", "col_1")
X_ROW = ("col_0", "row_1", "row_0")
Z_ROW = ("col_1", "row_1", "row_0")
N_ROW = 16
N_X = 4
N_Z = 8
N_COL = 32
HALF = FF // N_COL
WIDTH = FF // N_ROW
CHUNK = 64
SHIFT = HALF - (HALF // CHUNK) * CHUNK
BF16 = jnp.bfloat16
F32 = jnp.float32
VMEM_LIMIT = 48 * 1024 * 1024


def place_among(other, row):
    return (other * 2 + row % 2) * (N_ROW // 2) + row // 2


def low_lanes(rows):
    return lax.broadcasted_iota(jnp.int32, (rows, 128), 1) < 64


def swap_halves(tile):
    return pltpu.roll(tile, 64, 1)


def pack_kernel(
    acts_in, errs_in, cols_in, rows_in, mask_in,
    out_ref, cols_ref, rows_ref, mask_ref,
    acts_ref, errs_ref, padded, packed, sems,
):
    pairs = (
        (acts_in, acts_ref),
        (errs_in, errs_ref),
        (cols_in, cols_ref),
        (rows_in, rows_ref),
        (mask_in, mask_ref),
    )
    copies = [
        pltpu.make_async_copy(source, target, sems.at[i])
        for i, (source, target) in enumerate(pairs)
    ]
    for copy in copies:
        copy.start()
    for copy in copies:
        copy.wait()
    padded[...] = jnp.zeros_like(padded)
    padded[:, :HALF] = acts_ref[...].astype(F32)
    plain = padded[...]
    second_half = lax.rem(lax.axis_index("col_1"), 2) == 1
    acts = jnp.where(second_half, pltpu.roll(plain, SHIFT, 1), plain)
    errs = errs_ref[...].astype(F32)
    low = low_lanes(8)
    up = 32 * lax.div(lax.axis_index("col_1"), 2)
    lane = lax.broadcasted_iota(jnp.int32, (8, 128), 1)
    quarter = lane[:2] // 32
    err_tiles = []
    for z in range(N_Z):
        first = pltpu.roll(errs[:, :128], (128 - 16 * z) % 128, 1)
        second = pltpu.roll(errs[:, 128:], (144 - 16 * z) % 128, 1)
        both = jnp.where(lane < 16, first, second)
        tile = both[:2]
        for v in range(1, 4):
            turned = pltpu.roll(both, 32 * v, 1)
            tile = jnp.where(quarter == v, turned[2 * v : 2 * v + 2], tile)
        err_tiles.append(pltpu.roll(tile, 16 * lax.axis_index("row_0"), 1))
    for row in range(N_ROW):
        lanes = slice(128 * (row // 2), 128 * (row // 2) + 128)
        upper, lower = acts[:8, lanes], acts[8:, lanes]
        if row % 2 == 0:
            tile = jnp.where(low, upper, swap_halves(lower))
        else:
            tile = jnp.where(low, swap_halves(upper), lower)
        tile = pltpu.roll(tile, up, 1)
        for z in range(N_Z):
            start = place_among(z, row) * 10
            packed[start : start + 8, :] = tile
            packed[start + 8 : start + 10, :] = err_tiles[z]
    out_ref[...] = packed[: out_ref.shape[0], :].astype(BF16)


def gather_group(tiles, which):
    count = len(tiles)
    width = 128 // count
    rows = tiles[0].shape[0]
    wanted = lax.broadcasted_iota(jnp.int32, (rows, 128), 1) // width
    result = tiles[-which % count]
    for place in range(1, count):
        result = jnp.where(wanted == place, tiles[(place - which) % count], result)
    return pltpu.roll(result, 128 - width * which, 1) if which else result


def spread_kernel(in_ref, out_ref, packed):
    packed[: in_ref.shape[0], :] = in_ref[...].astype(F32)
    for pair in range(N_ROW // 2):
        for half in range(2):
            sources = []
            for row in (2 * pair, 2 * pair + 1):
                starts = [place_among(z, row) * 10 for z in range(half, N_Z, 2)]
                sources.append([packed[s : s + 8, :] for s in starts])
            for part in range(2):
                for q in range(2):
                    both = jnp.concatenate(
                        [gather_group(tiles, 2 * part + q) for tiles in sources], axis=0
                    )
                    start = 128 * part + 16 * pair
                    out_ref[2 * half + q, start : start + 16, :] = both.astype(BF16)
    for parity in range(2):
        pieces = [[], []]
        for part in range(2):
            sources = []
            for block in range(8):
                starts = [
                    place_among(z, 2 * block + parity) * 10 + 8
                    for z in range(part, N_Z, 2)
                ]
                sources.append(
                    jnp.concatenate([packed[s : s + 2, :] for s in starts], axis=0)
                )
            for v in range(4):
                for q in range(2):
                    pieces[q].append(gather_group(sources, 2 * v + q))
        for q in range(2):
            errs = jnp.concatenate(pieces[q], axis=0).astype(BF16)
            start = 256 + 64 * (2 * parity + q)
            for x in range(N_X):
                out_ref[x, start : start + 64, :] = errs


def node_value(index, count):
    return jnp.cos(jnp.pi * (2.0 * index.astype(F32) + 1.0) / (2.0 * count))


def parity_sign(count):
    return (1 - 2 * (count % 2)).astype(F32)


def mix_matrix(cols_ref, rows_ref, mask_ref):
    iota = functools.partial(lax.broadcasted_iota, jnp.int32)
    cols = cols_ref[...]
    rows = rows_ref[...]
    live = mask_ref[...]
    col_eye = iota((N_COL, N_COL), 0) == iota((N_COL, N_COL), 1)
    row_eye = iota((N_ROW, N_ROW), 0) == iota((N_ROW, N_ROW), 1)
    col_point = jnp.sum(jnp.where(col_eye, cols, 0), axis=1, keepdims=True)
    row_point = jnp.sum(jnp.where(row_eye, rows, 0), axis=1, keepdims=True)
    work_acts = node_value(col_point, 2 * N_COL + 1)
    work_errs = node_value(row_point, 2 * N_ROW + 1)
    row_rank = jnp.sum((rows < row_point).astype(jnp.int32), axis=1, keepdims=True)
    row_sign = parity_sign(row_rank)

    lane = iota((1, 128), 1)
    err_in, act_in = lane // 16, lane % 16
    term = parity_sign(err_in) / (work_errs - node_value(err_in, 8))
    total = jnp.sum(jnp.where(act_in == 0, term, 0.0), axis=1, keepdims=True)
    encode_errs = term / total
    term = parity_sign(act_in) / (work_acts - node_value(act_in, 16))
    total = jnp.sum(jnp.where(err_in == 0, term, 0.0), axis=1, keepdims=True)
    encode_acts = term / total
    act_out, err_out = lane // 8, lane % 8
    term = row_sign / (node_value(err_out, 8) - work_errs)
    decode_errs = term / jnp.sum(term, axis=0, keepdims=True)
    inverse = 1.0 / (node_value(act_out, 16) - work_acts)

    lower = cols < col_point
    left, right = [], []
    for i in range(N_ROW):
        here = live[i : i + 1, :]
        rank = jnp.sum(jnp.where(lower, here, 0), axis=1, keepdims=True)
        own = jnp.sum(jnp.where(col_eye, here, 0), axis=1, keepdims=True)
        term = (own.astype(F32) * parity_sign(rank)) * inverse
        decode = term / jnp.sum(term, axis=0, keepdims=True)
        left.append(decode * decode_errs[i : i + 1, :])
        right.append(encode_acts * encode_errs[i : i + 1, :])
    return lax.dot_general(
        jnp.concatenate(left, axis=0),
        jnp.concatenate(right, axis=0),
        (((0,), (0,)), ((), ())),
        preferred_element_type=F32,
        precision=lax.Precision.HIGHEST,
    ).astype(BF16)


def one_hot(source, size):
    here = lax.broadcasted_iota(jnp.int32, (size, size), 0)
    return jnp.where(here == source, 1.0, 0.0).astype(BF16)


def product_kernel(
    in_ref, cols_ref, rows_ref, mask_ref, out_ref, squares_ref, products
):
    to = lax.broadcasted_iota(jnp.int32, (256, 256), 1)
    tokens = one_hot(
        to // 32 * 32 + to // 2 % 4 * 8 + to // 8 % 4 * 2 + to % 2, 256
    )
    to = lax.broadcasted_iota(jnp.int32, (128, 128), 1)
    up = 2 * lax.axis_index("row_1") + lax.rem(lax.axis_index("col_0"), 2)
    features = one_hot(to % 8 * 16 + to // 8 % 4 * 4 + (to // 32 + 4 - up) % 4, 128)
    turned = []
    for target in range(N_X):
        errs = jnp.concatenate(
            [
                in_ref[x, start : start + 32, :]
                for start in (256 + 64 * target, 288 + 64 * target)
                for x in range(N_X)
            ],
            axis=0,
        )
        errs = jnp.dot(errs, features, preferred_element_type=F32).astype(BF16)
        turned.append(
            lax.dot_general(
                errs, tokens, (((0,), (0,)), ((), ())), preferred_element_type=F32
            ).astype(BF16)
        )
    errs = jnp.concatenate(
        [tile[32 * r : 32 * r + 32, :] for r in range(4) for tile in turned], axis=0
    )
    for x in range(0, N_X, 2):
        acts = jnp.concatenate([in_ref[x, :256, :], in_ref[x + 1, :256, :]], axis=1)
        product = jnp.dot(errs, acts, preferred_element_type=F32)
        for i in range(2):
            tiles = []
            for r in range(4):
                tile = product[128 * r : 128 * r + 128, 128 * i : 128 * i + 128]
                tiles.append(pltpu.roll(tile, 32 * r, 1) if r else tile)
            for z in range(4):
                where = pl.ds(4 * (x + i) + z, 128, stride=16)
                products[where, :] = gather_group(tiles, z)
    mix = mix_matrix(cols_ref, rows_ref, mask_ref)
    squares = jnp.zeros((128, 256), F32)
    for pair in range(8):
        both = [
            products[128 * s : 128 * s + 128, :].astype(BF16)
            for s in (2 * pair, 2 * pair + 1)
        ]
        grad = jnp.dot(mix, jnp.concatenate(both, axis=1), preferred_element_type=F32)
        squares = squares + grad * grad
        mixed = [grad[:, :128], grad[:, 128:]]
        start = 16 * (pair % 2)
        for k in range(N_ROW):
            both = jnp.concatenate(
                [grad[8 * k : 8 * k + 8, :] for grad in mixed], axis=0
            )
            out_ref[place_among(pair // 2, k), start : start + 16, :] = both.astype(BF16)
    squares_ref[...] = jnp.full(squares_ref.shape, jnp.sum(squares), F32)


def carry_kernel(in_ref, squares_ref, out_ref, packed):
    total = jnp.sum(squares_ref[...], axis=0)
    high = total.astype(BF16).astype(F32)
    middle = (total - high).astype(BF16).astype(F32)
    last = total - high - middle
    row = lax.broadcasted_iota(jnp.int32, (2, 128), 0)
    lane = lax.broadcasted_iota(jnp.int32, (2, 128), 1)
    rows = jnp.where(row == 0, high, jnp.where(lane < 64, middle, last))
    for peer in range(N_ROW * N_X):
        packed[34 * peer : 34 * peer + 32, :] = in_ref[peer].astype(F32)
        packed[34 * peer + 32 : 34 * peer + 34, :] = rows
    out_ref[...] = packed[: out_ref.shape[0], :].astype(BF16)


def place_kernel(in_ref, out_ref, packed, tile_ref, first_ref, second_ref, sems):
    packed[: in_ref.shape[0], :] = in_ref[...].astype(F32)
    squares = jnp.zeros((2, 128), F32)
    for peer in range(N_ROW * N_X):
        squares = squares + packed[34 * peer + 32 : 34 * peer + 34, :]
    squares = squares[:1, :1] + squares[1:, :1] + squares[1:, 64:65]
    factor = jnp.minimum(1.0, jnp.sqrt(jnp.float32(FF * D)) / jnp.sqrt(squares + 1e-06))

    copies = []
    for part, staged in enumerate((first_ref, second_ref)):
        for s in (2 * part, 2 * part + 1):
            for j in range(8):
                for half in range(2):
                    peers = [
                        place_among(2 * half + q, 2 * j + a) for a in range(2) for q in range(2)
                    ]
                    starts = [34 * peer + 8 * s for peer in peers]
                    tiles = [packed[start : start + 8, :] * factor for start in starts]
                    for r in range(4):
                        start = (4 * s + r) * 8
                        value = gather_group(tiles, r)
                        if half == 0 and j == 7:
                            value = value + tile_ref[7, start : start + 8, :]
                        tile_ref[j + 7 * half, start : start + 8, :] = value
        for tile in range(15):
            end = min(128 * tile + 128, WIDTH)
            for l in range(8):
                rows = tile_ref[tile, pl.ds(64 * part + l, 8, stride=8), :]
                staged[l, :, 128 * tile : end] = rows[:, : end - 128 * tile]
        copy = pltpu.make_async_copy(
            staged, out_ref.at[:, 8 * part : 8 * part + 8, :], sems.at[part]
        )
        copy.start()
        copies.append(copy)
    for copy in copies:
        copy.wait()


def vmem(count):
    return [pl.BlockSpec(memory_space=pltpu.VMEM) for _ in range(count)]


def call(kernel, out, in_specs, scratch=(), out_space=pltpu.VMEM):
    many = isinstance(out, tuple)
    return pl.pallas_call(
        kernel,
        out_shape=out,
        in_specs=in_specs,
        out_specs=tuple(vmem(len(out))) if many else pl.BlockSpec(memory_space=out_space),
        scratch_shapes=list(scratch),
        compiler_params=pltpu.CompilerParams(vmem_limit_bytes=VMEM_LIMIT),
    )


def shards(hidden_acts, output_errors, col_points, row_points, worker_mask):
    shape = jax.ShapeDtypeStruct
    args = (
        hidden_acts,
        output_errors,
        col_points[None, :],
        row_points[None, :],
        worker_mask,
    )
    points = tuple(shape(arg.shape, arg.dtype) for arg in args[2:])
    packed, *points = call(
        pack_kernel,
        (shape((N_ROW * N_Z * 10, 128), BF16), *points),
        [pl.BlockSpec(memory_space=pltpu.HBM)] * 5,
        [
            pltpu.VMEM((16, HALF), BF16),
            pltpu.VMEM((8, 256), BF16),
            pltpu.VMEM((16, 1024), F32),
            pltpu.VMEM((N_ROW * N_Z * 10 + 8, 128), F32),
            pltpu.SemaphoreType.DMA((5,)),
        ],
    )(*[pltpu.with_memory_space_constraint(arg, pltpu.HBM) for arg in args])
    packed = packed.reshape(N_ROW * N_Z, 5, 2, 128)
    packed = lax.all_to_all(packed, Z_ROW, 0, 0, tiled=True)
    spread = call(
        spread_kernel,
        shape((N_X, 512, 128), BF16),
        vmem(1),
        [pltpu.VMEM((N_ROW * N_Z * 10 + 8, 128), F32)],
    )(packed.reshape(N_ROW * N_Z * 10, 128))
    spread = lax.all_to_all(spread, "col_0", 0, 0, tiled=True)
    peers = N_ROW * N_X
    mixed, squares = call(
        product_kernel,
        (shape((peers, 32, 128), BF16), shape((N_Z, 1, 128), F32)),
        vmem(4),
        [pltpu.VMEM((2048 + 16, 128), F32)],
    )(spread, *points)
    squares = lax.all_to_all(squares, "col_1", 0, 0, tiled=True)
    mixed = call(
        carry_kernel,
        shape((peers * 34, 128), BF16),
        vmem(2),
        [pltpu.VMEM((peers * 34 + 8, 128), F32)],
    )(mixed, squares)
    mixed = lax.all_to_all(mixed.reshape(peers, 17, 2, 128), X_ROW, 0, 0, tiled=True)
    return call(
        place_kernel,
        shape((8, 16, WIDTH), F32),
        vmem(1),
        [
            pltpu.VMEM((peers * 34 + 8, 128), F32),
            pltpu.VMEM((15, 128 + 8, 128), F32),
            pltpu.VMEM((8, 8, WIDTH), F32),
            pltpu.VMEM((8, 8, WIDTH), F32),
            pltpu.SemaphoreType.DMA((2,)),
        ],
        pltpu.HBM,
    )(mixed.reshape(peers * 34, 128))


def solution(mesh):
    finer = Mesh(mesh.devices.reshape(8, 2, 4, 8), ROW + COL)
    in_specs = (P(ROW, COL), P(COL, ROW), P(), P(), P())
    return jax.shard_map(
        shards, mesh=finer, in_specs=in_specs, out_specs=P(None, COL, ROW), check_vma=False
    )
```

```python
import functools

import jax
import jax.numpy as jnp
from jax import lax
from jax.experimental import pallas as pl
from jax.experimental.pallas import tpu as pltpu
from jax.sharding import Mesh
from jax.sharding import PartitionSpec as P

D = 4096
FF = 29568
ROW = ("row_0", "row_1")
COL = ("col_0", "col_1")
X_ROW = ("col_0", "row_1", "row_0")
Z_ROW = ("col_1", "row_1", "row_0")
N_ROW = 16
N_X = 4
N_Z = 8
N_COL = 32
HALF = FF // N_COL
WIDTH = FF // N_ROW
CHUNK = 64
SHIFT = HALF - (HALF // CHUNK) * CHUNK
BF16 = jnp.bfloat16
F32 = jnp.float32
VMEM_LIMIT = 48 * 1024 * 1024


def place_among(other, row):
    return (other * 2 + row % 2) * (N_ROW // 2) + row // 2


def low_lanes(rows):
    return lax.broadcasted_iota(jnp.int32, (rows, 128), 1) < 64


def swap_halves(tile):
    return pltpu.roll(tile, 64, 1)


def pack_kernel(
    acts_in, errs_in, cols_in, rows_in, mask_in,
    out_ref, cols_ref, rows_ref, mask_ref,
    acts_ref, errs_ref, padded, packed, sems,
):
    pairs = (
        (acts_in, acts_ref),
        (errs_in, errs_ref),
        (cols_in, cols_ref),
        (rows_in, rows_ref),
        (mask_in, mask_ref),
    )
    copies = [
        pltpu.make_async_copy(source, target, sems.at[i])
        for i, (source, target) in enumerate(pairs)
    ]
    for copy in copies:
        copy.start()
    for copy in copies:
        copy.wait()
    padded[...] = jnp.zeros_like(padded)
    padded[:, :HALF] = acts_ref[...].astype(F32)
    plain = padded[...]
    second_half = lax.rem(lax.axis_index("col_1"), 2) == 1
    acts = jnp.where(second_half, pltpu.roll(plain, SHIFT, 1), plain)
    errs = errs_ref[...].astype(F32)
    low = low_lanes(8)
    up = 32 * lax.div(lax.axis_index("col_1"), 2)
    lane = lax.broadcasted_iota(jnp.int32, (8, 128), 1)
    quarter = lane[:2] // 32
    err_tiles = []
    for z in range(N_Z):
        first = pltpu.roll(errs[:, :128], (128 - 16 * z) % 128, 1)
        second = pltpu.roll(errs[:, 128:], (144 - 16 * z) % 128, 1)
        both = jnp.where(lane < 16, first, second)
        tile = both[:2]
        for v in range(1, 4):
            turned = pltpu.roll(both, 32 * v, 1)
            tile = jnp.where(quarter == v, turned[2 * v : 2 * v + 2], tile)
        err_tiles.append(pltpu.roll(tile, 16 * lax.axis_index("row_0"), 1))
    for row in range(N_ROW):
        lanes = slice(128 * (row // 2), 128 * (row // 2) + 128)
        upper, lower = acts[:8, lanes], acts[8:, lanes]
        if row % 2 == 0:
            tile = jnp.where(low, upper, swap_halves(lower))
        else:
            tile = jnp.where(low, swap_halves(upper), lower)
        tile = pltpu.roll(tile, up, 1)
        for z in range(N_Z):
            start = place_among(z, row) * 10
            packed[start : start + 8, :] = tile
            packed[start + 8 : start + 10, :] = err_tiles[z]
    out_ref[...] = packed[: out_ref.shape[0], :].astype(BF16)


def gather_groups(tiles):
    count = len(tiles)
    width = 128 // count
    rows = tiles[0].shape[0]
    group = lax.broadcasted_iota(jnp.int32, (rows, 128), 1) // width
    step = 1
    while step < count:
        later = group // step % 2 == 1
        tiles = [
            jnp.where(later, tiles[(i + step) % count], tiles[i]) for i in range(count)
        ]
        step *= 2
    results = [tiles[0]]
    for which in range(1, count):
        results.append(pltpu.roll(tiles[count - which], 128 - width * which, 1))
    return results


def spread_kernel(in_ref, out_ref, packed):
    packed[: in_ref.shape[0], :] = in_ref[...].astype(F32)
    for pair in range(N_ROW // 2):
        for half in range(2):
            sources = []
            for row in (2 * pair, 2 * pair + 1):
                starts = [place_among(z, row) * 10 for z in range(half, N_Z, 2)]
                sources.append(gather_groups([packed[s : s + 8, :] for s in starts]))
            for part in range(2):
                for q in range(2):
                    both = jnp.concatenate(
                        [tiles[2 * part + q] for tiles in sources], axis=0
                    )
                    start = 128 * part + 16 * pair
                    out_ref[2 * half + q, start : start + 16, :] = both.astype(BF16)
    for parity in range(2):
        pieces = [[], []]
        for part in range(2):
            sources = []
            for block in range(8):
                starts = [
                    place_among(z, 2 * block + parity) * 10 + 8
                    for z in range(part, N_Z, 2)
                ]
                sources.append(
                    jnp.concatenate([packed[s : s + 2, :] for s in starts], axis=0)
                )
            gathered = gather_groups(sources)
            for q in range(2):
                pieces[q] += gathered[q::2]
        for q in range(2):
            errs = jnp.concatenate(pieces[q], axis=0).astype(BF16)
            start = 256 + 64 * (2 * parity + q)
            for x in range(N_X):
                out_ref[x, start : start + 64, :] = errs


def node_value(index, count):
    return jnp.cos(jnp.pi * (2.0 * index.astype(F32) + 1.0) / (2.0 * count))


def parity_sign(count):
    return (1 - 2 * (count % 2)).astype(F32)


def mix_matrix(cols_ref, rows_ref, mask_ref):
    iota = functools.partial(lax.broadcasted_iota, jnp.int32)
    cols = cols_ref[...]
    rows = rows_ref[...]
    live = mask_ref[...]
    col_eye = iota((N_COL, N_COL), 0) == iota((N_COL, N_COL), 1)
    row_eye = iota((N_ROW, N_ROW), 0) == iota((N_ROW, N_ROW), 1)
    col_point = jnp.sum(jnp.where(col_eye, cols, 0), axis=1, keepdims=True)
    row_point = jnp.sum(jnp.where(row_eye, rows, 0), axis=1, keepdims=True)
    work_acts = node_value(col_point, 2 * N_COL + 1)
    work_errs = node_value(row_point, 2 * N_ROW + 1)
    row_rank = jnp.sum((rows < row_point).astype(jnp.int32), axis=1, keepdims=True)
    row_sign = parity_sign(row_rank)

    lane = iota((1, 128), 1)
    err_in, act_in = lane // 16, lane % 16
    term = parity_sign(err_in) / (work_errs - node_value(err_in, 8))
    total = jnp.sum(jnp.where(act_in == 0, term, 0.0), axis=1, keepdims=True)
    encode_errs = term / total
    term = parity_sign(act_in) / (work_acts - node_value(act_in, 16))
    total = jnp.sum(jnp.where(err_in == 0, term, 0.0), axis=1, keepdims=True)
    encode_acts = term / total
    act_out, err_out = lane // 8, lane % 8
    term = row_sign / (node_value(err_out, 8) - work_errs)
    decode_errs = term / jnp.sum(term, axis=0, keepdims=True)
    inverse = 1.0 / (node_value(act_out, 16) - work_acts)

    lower = cols < col_point
    left, right = [], []
    for i in range(N_ROW):
        here = live[i : i + 1, :]
        rank = jnp.sum(jnp.where(lower, here, 0), axis=1, keepdims=True)
        own = jnp.sum(jnp.where(col_eye, here, 0), axis=1, keepdims=True)
        term = (own.astype(F32) * parity_sign(rank)) * inverse
        decode = term / jnp.sum(term, axis=0, keepdims=True)
        left.append(decode * decode_errs[i : i + 1, :])
        right.append(encode_acts * encode_errs[i : i + 1, :])
    return lax.dot_general(
        jnp.concatenate(left, axis=0),
        jnp.concatenate(right, axis=0),
        (((0,), (0,)), ((), ())),
        preferred_element_type=F32,
        precision=lax.Precision.HIGHEST,
    ).astype(BF16)


def one_hot(source, size):
    here = lax.broadcasted_iota(jnp.int32, (size, size), 0)
    return jnp.where(here == source, 1.0, 0.0).astype(BF16)


def product_kernel(
    in_ref, cols_ref, rows_ref, mask_ref, out_ref, squares_ref, products
):
    to = lax.broadcasted_iota(jnp.int32, (256, 256), 1)
    tokens = one_hot(
        to // 32 * 32 + to // 2 % 4 * 8 + to // 8 % 4 * 2 + to % 2, 256
    )
    to = lax.broadcasted_iota(jnp.int32, (128, 128), 1)
    up = 2 * lax.axis_index("row_1") + lax.rem(lax.axis_index("col_0"), 2)
    features = one_hot(to % 8 * 16 + to // 8 % 4 * 4 + (to // 32 + 4 - up) % 4, 128)
    turned = []
    for target in range(N_X):
        errs = jnp.concatenate(
            [
                in_ref[x, start : start + 32, :]
                for start in (256 + 64 * target, 288 + 64 * target)
                for x in range(N_X)
            ],
            axis=0,
        )
        errs = jnp.dot(errs, features, preferred_element_type=F32).astype(BF16)
        turned.append(
            lax.dot_general(
                errs, tokens, (((0,), (0,)), ((), ())), preferred_element_type=F32
            ).astype(BF16)
        )
    errs = jnp.concatenate(
        [tile[32 * r : 32 * r + 32, :] for r in range(4) for tile in turned], axis=0
    )
    for x in range(0, N_X, 2):
        acts = jnp.concatenate([in_ref[x, :256, :], in_ref[x + 1, :256, :]], axis=1)
        product = jnp.dot(errs, acts, preferred_element_type=F32)
        for i in range(2):
            tiles = []
            for r in range(4):
                tile = product[128 * r : 128 * r + 128, 128 * i : 128 * i + 128]
                tiles.append(pltpu.roll(tile, 32 * r, 1) if r else tile)
            for z, tile in enumerate(gather_groups(tiles)):
                products[pl.ds(4 * (x + i) + z, 128, stride=16), :] = tile
        if x == 0:
            mix = mix_matrix(cols_ref, rows_ref, mask_ref)
    squares = jnp.zeros((128, 256), F32)
    for pair in range(8):
        both = [
            products[128 * s : 128 * s + 128, :].astype(BF16)
            for s in (2 * pair, 2 * pair + 1)
        ]
        grad = jnp.dot(mix, jnp.concatenate(both, axis=1), preferred_element_type=F32)
        squares = squares + grad * grad
        mixed = [grad[:, :128], grad[:, 128:]]
        start = 16 * (pair % 2)
        for k in range(N_ROW):
            both = jnp.concatenate(
                [grad[8 * k : 8 * k + 8, :] for grad in mixed], axis=0
            )
            out_ref[place_among(pair // 2, k), start : start + 16, :] = both.astype(BF16)
    squares_ref[...] = jnp.full(squares_ref.shape, jnp.sum(squares), F32)


def carry_kernel(in_ref, squares_ref, out_ref, packed):
    total = jnp.sum(squares_ref[...], axis=0)
    high = total.astype(BF16).astype(F32)
    middle = (total - high).astype(BF16).astype(F32)
    last = total - high - middle
    row = lax.broadcasted_iota(jnp.int32, (2, 128), 0)
    lane = lax.broadcasted_iota(jnp.int32, (2, 128), 1)
    rows = jnp.where(row == 0, high, jnp.where(lane < 64, middle, last))
    for peer in range(N_ROW * N_X):
        packed[34 * peer : 34 * peer + 32, :] = in_ref[peer].astype(F32)
        packed[34 * peer + 32 : 34 * peer + 34, :] = rows
    out_ref[...] = packed[: out_ref.shape[0], :].astype(BF16)


def place_kernel(in_ref, out_ref, packed, tile_ref, first_ref, second_ref, sems):
    packed[: in_ref.shape[0], :] = in_ref[...].astype(F32)
    squares = jnp.zeros((2, 128), F32)
    for peer in range(N_ROW * N_X):
        squares = squares + packed[34 * peer + 32 : 34 * peer + 34, :]
    squares = squares[:1, :1] + squares[1:, :1] + squares[1:, 64:65]
    factor = jnp.minimum(1.0, jnp.sqrt(jnp.float32(FF * D)) / jnp.sqrt(squares + 1e-06))

    copies = []
    for part, staged in enumerate((first_ref, second_ref)):
        for s in (2 * part, 2 * part + 1):
            for j in range(8):
                for half in range(2):
                    peers = [
                        place_among(2 * half + q, 2 * j + a) for a in range(2) for q in range(2)
                    ]
                    starts = [34 * peer + 8 * s for peer in peers]
                    tiles = [packed[start : start + 8, :] * factor for start in starts]
                    for r, value in enumerate(gather_groups(tiles)):
                        start = (4 * s + r) * 8
                        if half == 0 and j == 7:
                            value = value + tile_ref[7, start : start + 8, :]
                        tile_ref[j + 7 * half, start : start + 8, :] = value
        for tile in range(15):
            end = min(128 * tile + 128, WIDTH)
            for l in range(8):
                rows = tile_ref[tile, pl.ds(64 * part + l, 8, stride=8), :]
                staged[l, :, 128 * tile : end] = rows[:, : end - 128 * tile]
        copy = pltpu.make_async_copy(
            staged, out_ref.at[:, 8 * part : 8 * part + 8, :], sems.at[part]
        )
        copy.start()
        copies.append(copy)
    for copy in copies:
        copy.wait()


def vmem(count):
    return [pl.BlockSpec(memory_space=pltpu.VMEM) for _ in range(count)]


def call(kernel, out, in_specs, scratch=(), out_space=pltpu.VMEM):
    many = isinstance(out, tuple)
    return pl.pallas_call(
        kernel,
        out_shape=out,
        in_specs=in_specs,
        out_specs=tuple(vmem(len(out))) if many else pl.BlockSpec(memory_space=out_space),
        scratch_shapes=list(scratch),
        compiler_params=pltpu.CompilerParams(vmem_limit_bytes=VMEM_LIMIT),
    )


def shards(hidden_acts, output_errors, col_points, row_points, worker_mask):
    shape = jax.ShapeDtypeStruct
    args = (
        hidden_acts,
        output_errors,
        col_points[None, :],
        row_points[None, :],
        worker_mask,
    )
    points = tuple(shape(arg.shape, arg.dtype) for arg in args[2:])
    packed, *points = call(
        pack_kernel,
        (shape((N_ROW * N_Z * 10, 128), BF16), *points),
        [pl.BlockSpec(memory_space=pltpu.HBM)] * 5,
        [
            pltpu.VMEM((16, HALF), BF16),
            pltpu.VMEM((8, 256), BF16),
            pltpu.VMEM((16, 1024), F32),
            pltpu.VMEM((N_ROW * N_Z * 10 + 8, 128), F32),
            pltpu.SemaphoreType.DMA((5,)),
        ],
    )(*[pltpu.with_memory_space_constraint(arg, pltpu.HBM) for arg in args])
    packed = packed.reshape(N_ROW * N_Z, 5, 2, 128)
    packed = lax.all_to_all(packed, Z_ROW, 0, 0, tiled=True)
    spread = call(
        spread_kernel,
        shape((N_X, 512, 128), BF16),
        vmem(1),
        [pltpu.VMEM((N_ROW * N_Z * 10 + 8, 128), F32)],
    )(packed.reshape(N_ROW * N_Z * 10, 128))
    spread = lax.all_to_all(spread, "col_0", 0, 0, tiled=True)
    peers = N_ROW * N_X
    mixed, squares = call(
        product_kernel,
        (shape((peers, 32, 128), BF16), shape((N_Z, 1, 128), F32)),
        vmem(4),
        [pltpu.VMEM((2048 + 16, 128), F32)],
    )(spread, *points)
    squares = lax.all_to_all(squares, "col_1", 0, 0, tiled=True)
    mixed = call(
        carry_kernel,
        shape((peers * 34, 128), BF16),
        vmem(2),
        [pltpu.VMEM((peers * 34 + 8, 128), F32)],
    )(mixed, squares)
    mixed = lax.all_to_all(mixed.reshape(peers, 17, 2, 128), X_ROW, 0, 0, tiled=True)
    return call(
        place_kernel,
        shape((8, 16, WIDTH), F32),
        vmem(1),
        [
            pltpu.VMEM((peers * 34 + 8, 128), F32),
            pltpu.VMEM((15, 128 + 8, 128), F32),
            pltpu.VMEM((8, 8, WIDTH), F32),
            pltpu.VMEM((8, 8, WIDTH), F32),
            pltpu.SemaphoreType.DMA((2,)),
        ],
        pltpu.HBM,
    )(mixed.reshape(peers * 34, 128))


def solution(mesh):
    finer = Mesh(mesh.devices.reshape(8, 2, 4, 8), ROW + COL)
    in_specs = (P(ROW, COL), P(COL, ROW), P(), P(), P())
    return jax.shard_map(
        shards, mesh=finer, in_specs=in_specs, out_specs=P(None, COL, ROW), check_vma=False
    )
```

```python
import functools

import jax
import jax.numpy as jnp
from jax import lax
from jax.experimental import pallas as pl
from jax.experimental.pallas import tpu as pltpu
from jax.sharding import Mesh
from jax.sharding import PartitionSpec as P

D = 4096
FF = 29568
ROW = ("row_0", "row_1")
COL = ("col_0", "col_1")
X_ROW = ("col_0", "row_1", "row_0")
Z_ROW = ("col_1", "row_1", "row_0")
N_ROW = 16
N_X = 4
N_Z = 8
N_COL = 32
HALF = FF // N_COL
WIDTH = FF // N_ROW
CHUNK = 64
SHIFT = HALF - (HALF // CHUNK) * CHUNK
BF16 = jnp.bfloat16
F32 = jnp.float32
VMEM_LIMIT = 48 * 1024 * 1024


def place_among(other, row):
    return (other * 2 + row % 2) * (N_ROW // 2) + row // 2


def low_lanes(rows):
    return lax.broadcasted_iota(jnp.int32, (rows, 128), 1) < 64


def swap_halves(tile):
    return pltpu.roll(tile, 64, 1)


def pack_kernel(
    acts_in, errs_in, cols_in, rows_in, mask_in,
    out_ref, cols_ref, rows_ref, mask_ref,
    acts_ref, errs_ref, padded, packed, sems,
):
    pairs = (
        (acts_in, acts_ref),
        (errs_in, errs_ref),
        (cols_in, cols_ref),
        (rows_in, rows_ref),
        (mask_in, mask_ref),
    )
    copies = [
        pltpu.make_async_copy(source, target, sems.at[i])
        for i, (source, target) in enumerate(pairs)
    ]
    for copy in copies:
        copy.start()
    for copy in copies:
        copy.wait()
    padded[...] = jnp.zeros_like(padded)
    padded[:, :HALF] = acts_ref[...].astype(F32)
    plain = padded[...]
    second_half = lax.rem(lax.axis_index("col_1"), 2) == 1
    acts = jnp.where(second_half, pltpu.roll(plain, SHIFT, 1), plain)
    errs = errs_ref[...].astype(F32)
    low = low_lanes(8)
    up = 32 * lax.div(lax.axis_index("col_1"), 2)
    lane = lax.broadcasted_iota(jnp.int32, (8, 128), 1)
    quarter = lane[:2] // 32
    err_tiles = []
    for z in range(N_Z):
        first = pltpu.roll(errs[:, :128], (128 - 16 * z) % 128, 1)
        second = pltpu.roll(errs[:, 128:], (144 - 16 * z) % 128, 1)
        both = jnp.where(lane < 16, first, second)
        tile = both[:2]
        for v in range(1, 4):
            turned = pltpu.roll(both, 32 * v, 1)
            tile = jnp.where(quarter == v, turned[2 * v : 2 * v + 2], tile)
        err_tiles.append(pltpu.roll(tile, 16 * lax.axis_index("row_0"), 1))
    for row in range(N_ROW):
        lanes = slice(128 * (row // 2), 128 * (row // 2) + 128)
        upper, lower = acts[:8, lanes], acts[8:, lanes]
        if row % 2 == 0:
            tile = jnp.where(low, upper, swap_halves(lower))
        else:
            tile = jnp.where(low, swap_halves(upper), lower)
        tile = pltpu.roll(tile, up, 1)
        for z in range(N_Z):
            start = place_among(z, row) * 10
            packed[start : start + 8, :] = tile
            packed[start + 8 : start + 10, :] = err_tiles[z]
    out_ref[...] = packed[: out_ref.shape[0], :].astype(BF16)


def gather_groups(tiles):
    count = len(tiles)
    width = 128 // count
    rows = tiles[0].shape[0]
    group = lax.broadcasted_iota(jnp.int32, (rows, 128), 1) // width
    step = 1
    while step < count:
        later = group // step % 2 == 1
        tiles = [
            jnp.where(later, tiles[(i + step) % count], tiles[i]) for i in range(count)
        ]
        step *= 2
    results = [tiles[0]]
    for which in range(1, count):
        results.append(pltpu.roll(tiles[count - which], 128 - width * which, 1))
    return results


def spread_kernel(in_ref, out_ref, packed):
    packed[: in_ref.shape[0], :] = in_ref[...].astype(F32)
    for pair in range(N_ROW // 2):
        for half in range(2):
            sources = []
            for row in (2 * pair, 2 * pair + 1):
                starts = [place_among(z, row) * 10 for z in range(half, N_Z, 2)]
                sources.append(gather_groups([packed[s : s + 8, :] for s in starts]))
            for part in range(2):
                for q in range(2):
                    both = jnp.concatenate(
                        [tiles[2 * part + q] for tiles in sources], axis=0
                    )
                    start = 128 * part + 16 * pair
                    out_ref[2 * half + q, start : start + 16, :] = both.astype(BF16)
    for parity in range(2):
        pieces = [[], []]
        for part in range(2):
            sources = []
            for block in range(8):
                starts = [
                    place_among(z, 2 * block + parity) * 10 + 8
                    for z in range(part, N_Z, 2)
                ]
                sources.append(
                    jnp.concatenate([packed[s : s + 2, :] for s in starts], axis=0)
                )
            gathered = gather_groups(sources)
            for q in range(2):
                pieces[q] += gathered[q::2]
        for q in range(2):
            errs = jnp.concatenate(pieces[q], axis=0).astype(BF16)
            start = 256 + 64 * (2 * parity + q)
            for x in range(N_X):
                out_ref[x, start : start + 64, :] = errs


def node_value(index, count):
    return jnp.cos(jnp.pi * (2.0 * index.astype(F32) + 1.0) / (2.0 * count))


def parity_sign(count):
    return (1 - 2 * (count % 2)).astype(F32)


def mix_matrix(cols_ref, rows_ref, mask_ref):
    iota = functools.partial(lax.broadcasted_iota, jnp.int32)
    cols = cols_ref[...]
    rows = rows_ref[...]
    live = mask_ref[...]
    col_eye = iota((N_COL, N_COL), 0) == iota((N_COL, N_COL), 1)
    row_eye = iota((N_ROW, N_ROW), 0) == iota((N_ROW, N_ROW), 1)
    col_point = jnp.sum(jnp.where(col_eye, cols, 0), axis=1, keepdims=True)
    row_point = jnp.sum(jnp.where(row_eye, rows, 0), axis=1, keepdims=True)
    work_acts = node_value(col_point, 2 * N_COL + 1)
    work_errs = node_value(row_point, 2 * N_ROW + 1)
    row_rank = jnp.sum((rows < row_point).astype(jnp.int32), axis=1, keepdims=True)
    row_sign = parity_sign(row_rank)

    lane = iota((1, 128), 1)
    err_in, act_in = lane // 16, lane % 16
    term = parity_sign(err_in) / (work_errs - node_value(err_in, 8))
    total = jnp.sum(jnp.where(act_in == 0, term, 0.0), axis=1, keepdims=True)
    encode_errs = term / total
    term = parity_sign(act_in) / (work_acts - node_value(act_in, 16))
    total = jnp.sum(jnp.where(err_in == 0, term, 0.0), axis=1, keepdims=True)
    encode_acts = term / total
    act_out, err_out = lane // 8, lane % 8
    term = row_sign / (node_value(err_out, 8) - work_errs)
    decode_errs = term / jnp.sum(term, axis=0, keepdims=True)
    inverse = 1.0 / (node_value(act_out, 16) - work_acts)

    lower = cols < col_point
    left, right = [], []
    for i in range(N_ROW):
        here = live[i : i + 1, :]
        rank = jnp.sum(jnp.where(lower, here, 0), axis=1, keepdims=True)
        own = jnp.sum(jnp.where(col_eye, here, 0), axis=1, keepdims=True)
        term = (own.astype(F32) * parity_sign(rank)) * inverse
        decode = term / jnp.sum(term, axis=0, keepdims=True)
        left.append(decode * decode_errs[i : i + 1, :])
        right.append(encode_acts * encode_errs[i : i + 1, :])
    left, right = jnp.concatenate(left, axis=0), jnp.concatenate(right, axis=0)
    left_high, right_high = left.astype(BF16), right.astype(BF16)
    left_low = (left - left_high.astype(F32)).astype(BF16)
    right_low = (right - right_high.astype(F32)).astype(BF16)
    both = lax.dot_general(
        left_high,
        jnp.concatenate([right_high, right_low], axis=1),
        (((0,), (0,)), ((), ())),
        preferred_element_type=F32,
    )
    rest = lax.dot_general(
        left_low, right_high, (((0,), (0,)), ((), ())), preferred_element_type=F32
    )
    return (both[:, :128] + (both[:, 128:] + rest)).astype(BF16)


def one_hot(source, size):
    here = lax.broadcasted_iota(jnp.int32, (size, size), 0)
    return jnp.where(here == source, 1.0, 0.0).astype(BF16)


def product_kernel(
    in_ref, cols_ref, rows_ref, mask_ref, out_ref, squares_ref, products
):
    to = lax.broadcasted_iota(jnp.int32, (256, 256), 1)
    tokens = one_hot(
        to // 32 * 32 + to // 2 % 4 * 8 + to // 8 % 4 * 2 + to % 2, 256
    )
    to = lax.broadcasted_iota(jnp.int32, (128, 128), 1)
    up = 2 * lax.axis_index("row_1") + lax.rem(lax.axis_index("col_0"), 2)
    features = one_hot(to % 8 * 16 + to // 8 % 4 * 4 + (to // 32 + 4 - up) % 4, 128)
    turned = []
    for target in range(N_X):
        errs = jnp.concatenate(
            [
                in_ref[x, start : start + 32, :]
                for start in (256 + 64 * target, 288 + 64 * target)
                for x in range(N_X)
            ],
            axis=0,
        )
        errs = jnp.dot(errs, features, preferred_element_type=F32).astype(BF16)
        turned.append(
            lax.dot_general(
                errs, tokens, (((0,), (0,)), ((), ())), preferred_element_type=F32
            ).astype(BF16)
        )
    errs = jnp.concatenate(
        [tile[32 * r : 32 * r + 32, :] for r in range(4) for tile in turned], axis=0
    )
    for x in range(0, N_X, 2):
        acts = jnp.concatenate([in_ref[x, :256, :], in_ref[x + 1, :256, :]], axis=1)
        product = jnp.dot(errs, acts, preferred_element_type=F32)
        for i in range(2):
            tiles = []
            for r in range(4):
                tile = product[128 * r : 128 * r + 128, 128 * i : 128 * i + 128]
                tiles.append(pltpu.roll(tile, 32 * r, 1) if r else tile)
            for z, tile in enumerate(gather_groups(tiles)):
                products[pl.ds(4 * (x + i) + z, 128, stride=16), :] = tile
        if x == 0:
            mix = mix_matrix(cols_ref, rows_ref, mask_ref)
    squares = jnp.zeros((128, 256), F32)
    for pair in range(8):
        both = [
            products[128 * s : 128 * s + 128, :].astype(BF16)
            for s in (2 * pair, 2 * pair + 1)
        ]
        grad = jnp.dot(mix, jnp.concatenate(both, axis=1), preferred_element_type=F32)
        squares = squares + grad * grad
        mixed = [grad[:, :128], grad[:, 128:]]
        start = 16 * (pair % 2)
        for k in range(N_ROW):
            both = jnp.concatenate(
                [grad[8 * k : 8 * k + 8, :] for grad in mixed], axis=0
            )
            out_ref[place_among(pair // 2, k), start : start + 16, :] = both.astype(BF16)
    squares_ref[...] = jnp.full(squares_ref.shape, jnp.sum(squares), F32)


def carry_kernel(in_ref, squares_ref, out_ref, packed):
    total = jnp.sum(squares_ref[...], axis=0)
    high = total.astype(BF16).astype(F32)
    middle = (total - high).astype(BF16).astype(F32)
    last = total - high - middle
    row = lax.broadcasted_iota(jnp.int32, (2, 128), 0)
    lane = lax.broadcasted_iota(jnp.int32, (2, 128), 1)
    rows = jnp.where(row == 0, high, jnp.where(lane < 64, middle, last))
    for peer in range(N_ROW * N_X):
        packed[34 * peer : 34 * peer + 32, :] = in_ref[peer].astype(F32)
        packed[34 * peer + 32 : 34 * peer + 34, :] = rows
    out_ref[...] = packed[: out_ref.shape[0], :].astype(BF16)


def place_kernel(in_ref, out_ref, packed, tile_ref, first_ref, second_ref, sems):
    packed[: in_ref.shape[0], :] = in_ref[...].astype(F32)
    squares = jnp.zeros((2, 128), F32)
    for peer in range(N_ROW * N_X):
        squares = squares + packed[34 * peer + 32 : 34 * peer + 34, :]
    squares = squares[:1, :1] + squares[1:, :1] + squares[1:, 64:65]
    factor = jnp.minimum(1.0, jnp.sqrt(jnp.float32(FF * D)) / jnp.sqrt(squares + 1e-06))

    copies = []
    for part, staged in enumerate((first_ref, second_ref)):
        for s in (2 * part, 2 * part + 1):
            for j in range(8):
                for half in range(2):
                    peers = [
                        place_among(2 * half + q, 2 * j + a) for a in range(2) for q in range(2)
                    ]
                    starts = [34 * peer + 8 * s for peer in peers]
                    tiles = [packed[start : start + 8, :] * factor for start in starts]
                    for r, value in enumerate(gather_groups(tiles)):
                        start = (4 * s + r) * 8
                        if half == 0 and j == 7:
                            value = value + tile_ref[7, start : start + 8, :]
                        tile_ref[j + 7 * half, start : start + 8, :] = value
        for tile in range(15):
            end = min(128 * tile + 128, WIDTH)
            for l in range(8):
                rows = tile_ref[tile, pl.ds(64 * part + l, 8, stride=8), :]
                staged[l, :, 128 * tile : end] = rows[:, : end - 128 * tile]
        copy = pltpu.make_async_copy(
            staged, out_ref.at[:, 8 * part : 8 * part + 8, :], sems.at[part]
        )
        copy.start()
        copies.append(copy)
    for copy in copies:
        copy.wait()


def vmem(count):
    return [pl.BlockSpec(memory_space=pltpu.VMEM) for _ in range(count)]


def call(kernel, out, in_specs, scratch=(), out_space=pltpu.VMEM):
    many = isinstance(out, tuple)
    return pl.pallas_call(
        kernel,
        out_shape=out,
        in_specs=in_specs,
        out_specs=tuple(vmem(len(out))) if many else pl.BlockSpec(memory_space=out_space),
        scratch_shapes=list(scratch),
        compiler_params=pltpu.CompilerParams(vmem_limit_bytes=VMEM_LIMIT),
    )


def shards(hidden_acts, output_errors, col_points, row_points, worker_mask):
    shape = jax.ShapeDtypeStruct
    args = (
        hidden_acts,
        output_errors,
        col_points[None, :],
        row_points[None, :],
        worker_mask,
    )
    points = tuple(shape(arg.shape, arg.dtype) for arg in args[2:])
    packed, *points = call(
        pack_kernel,
        (shape((N_ROW * N_Z * 10, 128), BF16), *points),
        [pl.BlockSpec(memory_space=pltpu.HBM)] * 5,
        [
            pltpu.VMEM((16, HALF), BF16),
            pltpu.VMEM((8, 256), BF16),
            pltpu.VMEM((16, 1024), F32),
            pltpu.VMEM((N_ROW * N_Z * 10 + 8, 128), F32),
            pltpu.SemaphoreType.DMA((5,)),
        ],
    )(*[pltpu.with_memory_space_constraint(arg, pltpu.HBM) for arg in args])
    packed = packed.reshape(N_ROW * N_Z, 5, 2, 128)
    packed = lax.all_to_all(packed, Z_ROW, 0, 0, tiled=True)
    spread = call(
        spread_kernel,
        shape((N_X, 512, 128), BF16),
        vmem(1),
        [pltpu.VMEM((N_ROW * N_Z * 10 + 8, 128), F32)],
    )(packed.reshape(N_ROW * N_Z * 10, 128))
    spread = lax.all_to_all(spread, "col_0", 0, 0, tiled=True)
    peers = N_ROW * N_X
    mixed, squares = call(
        product_kernel,
        (shape((peers, 32, 128), BF16), shape((N_Z, 1, 128), F32)),
        vmem(4),
        [pltpu.VMEM((2048 + 16, 128), F32)],
    )(spread, *points)
    squares = lax.all_to_all(squares, "col_1", 0, 0, tiled=True)
    mixed = call(
        carry_kernel,
        shape((peers * 34, 128), BF16),
        vmem(2),
        [pltpu.VMEM((peers * 34 + 8, 128), F32)],
    )(mixed, squares)
    mixed = lax.all_to_all(mixed.reshape(peers, 17, 2, 128), X_ROW, 0, 0, tiled=True)
    return call(
        place_kernel,
        shape((8, 16, WIDTH), F32),
        vmem(1),
        [
            pltpu.VMEM((peers * 34 + 8, 128), F32),
            pltpu.VMEM((15, 128 + 8, 128), F32),
            pltpu.VMEM((8, 8, WIDTH), F32),
            pltpu.VMEM((8, 8, WIDTH), F32),
            pltpu.SemaphoreType.DMA((2,)),
        ],
        pltpu.HBM,
    )(mixed.reshape(peers * 34, 128))


def solution(mesh):
    finer = Mesh(mesh.devices.reshape(8, 2, 4, 8), ROW + COL)
    in_specs = (P(ROW, COL), P(COL, ROW), P(), P(), P())
    return jax.shard_map(
        shards, mesh=finer, in_specs=in_specs, out_specs=P(None, COL, ROW), check_vma=False
    )
```

```python
import functools

import jax
import jax.numpy as jnp
from jax import lax
from jax.experimental import pallas as pl
from jax.experimental.pallas import tpu as pltpu
from jax.sharding import Mesh
from jax.sharding import PartitionSpec as P

D = 4096
FF = 29568
ROW = ("row_0", "row_1")
COL = ("col_0", "col_1")
X_ROW = ("col_0", "row_1", "row_0")
Z_ROW = ("col_1", "row_1", "row_0")
N_ROW = 16
N_X = 4
N_Z = 8
N_COL = 32
HALF = FF // N_COL
WIDTH = FF // N_ROW
CHUNK = 64
SHIFT = HALF - (HALF // CHUNK) * CHUNK
BF16 = jnp.bfloat16
F32 = jnp.float32
VMEM_LIMIT = 48 * 1024 * 1024


def place_among(other, row):
    return (other * 2 + row % 2) * (N_ROW // 2) + row // 2


def low_lanes(rows):
    return lax.broadcasted_iota(jnp.int32, (rows, 128), 1) < 64


def swap_halves(tile):
    return pltpu.roll(tile, 64, 1)


def pack_kernel(
    acts_in, errs_in, cols_in, rows_in, mask_in,
    out_ref, cols_ref, rows_ref, mask_ref,
    acts_ref, errs_ref, padded, packed, sems,
):
    pairs = (
        (acts_in, acts_ref),
        (errs_in, errs_ref),
        (cols_in, cols_ref),
        (rows_in, rows_ref),
        (mask_in, mask_ref),
    )
    copies = [
        pltpu.make_async_copy(source, target, sems.at[i])
        for i, (source, target) in enumerate(pairs)
    ]
    for copy in copies:
        copy.start()
    copies[1].wait()
    errs = errs_ref[...].astype(F32)
    low = low_lanes(8)
    lane = lax.broadcasted_iota(jnp.int32, (8, 128), 1)
    quarter = lane[:2] // 32
    err_tiles = []
    for z in range(N_Z):
        first = pltpu.roll(errs[:, :128], (128 - 16 * z) % 128, 1)
        second = pltpu.roll(errs[:, 128:], (144 - 16 * z) % 128, 1)
        both = jnp.where(lane < 16, first, second)
        tile = both[:2]
        for v in range(1, 4):
            turned = pltpu.roll(both, 32 * v, 1)
            tile = jnp.where(quarter == v, turned[2 * v : 2 * v + 2], tile)
        err_tiles.append(pltpu.roll(tile, 16 * lax.axis_index("row_0"), 1))
    padded[...] = jnp.zeros_like(padded)
    copies[0].wait()
    padded[:, :HALF] = acts_ref[...].astype(F32)
    plain = padded[...]
    second_half = lax.rem(lax.axis_index("col_1"), 2) == 1
    acts = jnp.where(second_half, pltpu.roll(plain, SHIFT, 1), plain)
    up = 32 * lax.div(lax.axis_index("col_1"), 2)
    for row in range(N_ROW):
        lanes = slice(128 * (row // 2), 128 * (row // 2) + 128)
        upper, lower = acts[:8, lanes], acts[8:, lanes]
        if row % 2 == 0:
            tile = jnp.where(low, upper, swap_halves(lower))
        else:
            tile = jnp.where(low, swap_halves(upper), lower)
        tile = pltpu.roll(tile, up, 1)
        for z in range(N_Z):
            start = place_among(z, row) * 10
            packed[start : start + 8, :] = tile
            packed[start + 8 : start + 10, :] = err_tiles[z]
    out_ref[...] = packed[: out_ref.shape[0], :].astype(BF16)
    for copy in copies[2:]:
        copy.wait()


def gather_groups(tiles):
    count = len(tiles)
    width = 128 // count
    rows = tiles[0].shape[0]
    group = lax.broadcasted_iota(jnp.int32, (rows, 128), 1) // width
    step = 1
    while step < count:
        later = group // step % 2 == 1
        tiles = [
            jnp.where(later, tiles[(i + step) % count], tiles[i]) for i in range(count)
        ]
        step *= 2
    results = [tiles[0]]
    for which in range(1, count):
        results.append(pltpu.roll(tiles[count - which], 128 - width * which, 1))
    return results


def spread_kernel(in_ref, out_ref, packed):
    packed[: in_ref.shape[0], :] = in_ref[...].astype(F32)
    for pair in range(N_ROW // 2):
        for half in range(2):
            sources = []
            for row in (2 * pair, 2 * pair + 1):
                starts = [place_among(z, row) * 10 for z in range(half, N_Z, 2)]
                sources.append(gather_groups([packed[s : s + 8, :] for s in starts]))
            for part in range(2):
                for q in range(2):
                    both = jnp.concatenate(
                        [tiles[2 * part + q] for tiles in sources], axis=0
                    )
                    start = 128 * part + 16 * pair
                    out_ref[2 * half + q, start : start + 16, :] = both.astype(BF16)
    for parity in range(2):
        pieces = [[], []]
        for part in range(2):
            sources = []
            for block in range(8):
                starts = [
                    place_among(z, 2 * block + parity) * 10 + 8
                    for z in range(part, N_Z, 2)
                ]
                sources.append(
                    jnp.concatenate([packed[s : s + 2, :] for s in starts], axis=0)
                )
            gathered = gather_groups(sources)
            for q in range(2):
                pieces[q] += gathered[q::2]
        for q in range(2):
            errs = jnp.concatenate(pieces[q], axis=0).astype(BF16)
            start = 256 + 64 * (2 * parity + q)
            for x in range(N_X):
                out_ref[x, start : start + 64, :] = errs


def node_value(index, count):
    return jnp.cos(jnp.pi * (2.0 * index.astype(F32) + 1.0) / (2.0 * count))


def parity_sign(count):
    return (1 - 2 * (count % 2)).astype(F32)


def mix_matrix(cols_ref, rows_ref, mask_ref):
    iota = functools.partial(lax.broadcasted_iota, jnp.int32)
    cols = cols_ref[...]
    rows = rows_ref[...]
    live = mask_ref[...]
    col_eye = iota((N_COL, N_COL), 0) == iota((N_COL, N_COL), 1)
    row_eye = iota((N_ROW, N_ROW), 0) == iota((N_ROW, N_ROW), 1)
    col_point = jnp.sum(jnp.where(col_eye, cols, 0), axis=1, keepdims=True)
    row_point = jnp.sum(jnp.where(row_eye, rows, 0), axis=1, keepdims=True)
    work_acts = node_value(col_point, 2 * N_COL + 1)
    work_errs = node_value(row_point, 2 * N_ROW + 1)
    row_rank = jnp.sum((rows < row_point).astype(jnp.int32), axis=1, keepdims=True)
    row_sign = parity_sign(row_rank)

    lane = iota((1, 128), 1)
    err_in, act_in = lane // 16, lane % 16
    term = parity_sign(err_in) / (work_errs - node_value(err_in, 8))
    total = jnp.sum(jnp.where(act_in == 0, term, 0.0), axis=1, keepdims=True)
    encode_errs = term / total
    term = parity_sign(act_in) / (work_acts - node_value(act_in, 16))
    total = jnp.sum(jnp.where(err_in == 0, term, 0.0), axis=1, keepdims=True)
    encode_acts = term / total
    act_out, err_out = lane // 8, lane % 8
    term = row_sign / (node_value(err_out, 8) - work_errs)
    decode_errs = term / jnp.sum(term, axis=0, keepdims=True)
    inverse = 1.0 / (node_value(act_out, 16) - work_acts)

    lower = cols < col_point
    left, right = [], []
    for i in range(N_ROW):
        here = live[i : i + 1, :]
        rank = jnp.sum(jnp.where(lower, here, 0), axis=1, keepdims=True)
        own = jnp.sum(jnp.where(col_eye, here, 0), axis=1, keepdims=True)
        term = (own.astype(F32) * parity_sign(rank)) * inverse
        decode = term / jnp.sum(term, axis=0, keepdims=True)
        left.append(decode * decode_errs[i : i + 1, :])
        right.append(encode_acts * encode_errs[i : i + 1, :])
    left, right = jnp.concatenate(left, axis=0), jnp.concatenate(right, axis=0)
    left_high, right_high = left.astype(BF16), right.astype(BF16)
    left_low = (left - left_high.astype(F32)).astype(BF16)
    right_low = (right - right_high.astype(F32)).astype(BF16)
    both = lax.dot_general(
        left_high,
        jnp.concatenate([right_high, right_low], axis=1),
        (((0,), (0,)), ((), ())),
        preferred_element_type=F32,
    )
    rest = lax.dot_general(
        left_low, right_high, (((0,), (0,)), ((), ())), preferred_element_type=F32
    )
    return (both[:, :128] + (both[:, 128:] + rest)).astype(BF16)


def one_hot(source, size):
    here = lax.broadcasted_iota(jnp.int32, (size, size), 0)
    return jnp.where(here == source, 1.0, 0.0).astype(BF16)


def product_kernel(
    in_ref, cols_ref, rows_ref, mask_ref, out_ref, squares_ref, products
):
    to = lax.broadcasted_iota(jnp.int32, (256, 256), 1)
    tokens = one_hot(
        to // 32 * 32 + to // 2 % 4 * 8 + to // 8 % 4 * 2 + to % 2, 256
    )
    to = lax.broadcasted_iota(jnp.int32, (128, 128), 1)
    up = 2 * lax.axis_index("row_1") + lax.rem(lax.axis_index("col_0"), 2)
    features = one_hot(to % 8 * 16 + to // 8 % 4 * 4 + (to // 32 + 4 - up) % 4, 128)
    turned = []
    for target in range(N_X):
        errs = jnp.concatenate(
            [
                in_ref[x, start : start + 32, :]
                for start in (256 + 64 * target, 288 + 64 * target)
                for x in range(N_X)
            ],
            axis=0,
        )
        errs = jnp.dot(errs, features, preferred_element_type=F32).astype(BF16)
        turned.append(
            lax.dot_general(
                errs, tokens, (((0,), (0,)), ((), ())), preferred_element_type=F32
            ).astype(BF16)
        )
    errs = jnp.concatenate(
        [tile[32 * r : 32 * r + 32, :] for r in range(4) for tile in turned], axis=0
    )
    for x in range(0, N_X, 2):
        acts = jnp.concatenate([in_ref[x, :256, :], in_ref[x + 1, :256, :]], axis=1)
        product = jnp.dot(errs, acts, preferred_element_type=F32)
        for i in range(2):
            tiles = []
            for r in range(4):
                tile = product[128 * r : 128 * r + 128, 128 * i : 128 * i + 128]
                tiles.append(pltpu.roll(tile, 32 * r, 1) if r else tile)
            for z, tile in enumerate(gather_groups(tiles)):
                products[pl.ds(4 * (x + i) + z, 128, stride=16), :] = tile
        if x == 0:
            mix = mix_matrix(cols_ref, rows_ref, mask_ref)
    squares = jnp.zeros((128, 256), F32)
    for pair in range(8):
        both = [
            products[128 * s : 128 * s + 128, :].astype(BF16)
            for s in (2 * pair, 2 * pair + 1)
        ]
        grad = jnp.dot(mix, jnp.concatenate(both, axis=1), preferred_element_type=F32)
        squares = squares + grad * grad
        mixed = [grad[:, :128], grad[:, 128:]]
        start = 16 * (pair % 2)
        for k in range(N_ROW):
            both = jnp.concatenate(
                [grad[8 * k : 8 * k + 8, :] for grad in mixed], axis=0
            )
            out_ref[place_among(pair // 2, k), start : start + 16, :] = both.astype(BF16)
    squares_ref[...] = jnp.full(squares_ref.shape, jnp.sum(squares), F32)


def carry_kernel(in_ref, squares_ref, out_ref, packed):
    total = jnp.sum(squares_ref[...], axis=0)
    high = total.astype(BF16).astype(F32)
    middle = (total - high).astype(BF16).astype(F32)
    last = total - high - middle
    row = lax.broadcasted_iota(jnp.int32, (2, 128), 0)
    lane = lax.broadcasted_iota(jnp.int32, (2, 128), 1)
    rows = jnp.where(row == 0, high, jnp.where(lane < 64, middle, last))
    for peer in range(N_ROW * N_X):
        packed[34 * peer : 34 * peer + 32, :] = in_ref[peer].astype(F32)
        packed[34 * peer + 32 : 34 * peer + 34, :] = rows
    out_ref[...] = packed[: out_ref.shape[0], :].astype(BF16)


def place_kernel(in_ref, out_ref, packed, tile_ref, first_ref, second_ref, sems):
    packed[: in_ref.shape[0], :] = in_ref[...].astype(F32)
    squares = jnp.zeros((2, 128), F32)
    for peer in range(N_ROW * N_X):
        squares = squares + packed[34 * peer + 32 : 34 * peer + 34, :]
    squares = squares[:1, :1] + squares[1:, :1] + squares[1:, 64:65]
    factor = jnp.minimum(1.0, jnp.sqrt(jnp.float32(FF * D)) / jnp.sqrt(squares + 1e-06))

    copies = []
    for part, staged in enumerate((first_ref, second_ref)):
        for s in (2 * part, 2 * part + 1):
            for j in range(8):
                for half in range(2):
                    peers = [
                        place_among(2 * half + q, 2 * j + a) for a in range(2) for q in range(2)
                    ]
                    starts = [34 * peer + 8 * s for peer in peers]
                    tiles = [packed[start : start + 8, :] * factor for start in starts]
                    for r, value in enumerate(gather_groups(tiles)):
                        start = (4 * s + r) * 8
                        if half == 0 and j == 7:
                            value = value + tile_ref[7, start : start + 8, :]
                        tile_ref[j + 7 * half, start : start + 8, :] = value
        for tile in range(15):
            end = min(128 * tile + 128, WIDTH)
            for l in range(8):
                rows = tile_ref[tile, pl.ds(64 * part + l, 8, stride=8), :]
                staged[l, :, 128 * tile : end] = rows[:, : end - 128 * tile]
        copy = pltpu.make_async_copy(
            staged, out_ref.at[:, 8 * part : 8 * part + 8, :], sems.at[part]
        )
        copy.start()
        copies.append(copy)
    for copy in copies:
        copy.wait()


def vmem(count):
    return [pl.BlockSpec(memory_space=pltpu.VMEM) for _ in range(count)]


def call(kernel, out, in_specs, scratch=(), out_space=pltpu.VMEM):
    many = isinstance(out, tuple)
    return pl.pallas_call(
        kernel,
        out_shape=out,
        in_specs=in_specs,
        out_specs=tuple(vmem(len(out))) if many else pl.BlockSpec(memory_space=out_space),
        scratch_shapes=list(scratch),
        compiler_params=pltpu.CompilerParams(vmem_limit_bytes=VMEM_LIMIT),
    )


def shards(hidden_acts, output_errors, col_points, row_points, worker_mask):
    shape = jax.ShapeDtypeStruct
    args = (
        hidden_acts,
        output_errors,
        col_points[None, :],
        row_points[None, :],
        worker_mask,
    )
    points = tuple(shape(arg.shape, arg.dtype) for arg in args[2:])
    packed, *points = call(
        pack_kernel,
        (shape((N_ROW * N_Z * 10, 128), BF16), *points),
        [pl.BlockSpec(memory_space=pltpu.HBM)] * 5,
        [
            pltpu.VMEM((16, HALF), BF16),
            pltpu.VMEM((8, 256), BF16),
            pltpu.VMEM((16, 1024), F32),
            pltpu.VMEM((N_ROW * N_Z * 10 + 8, 128), F32),
            pltpu.SemaphoreType.DMA((5,)),
        ],
    )(*[pltpu.with_memory_space_constraint(arg, pltpu.HBM) for arg in args])
    packed = packed.reshape(N_ROW * N_Z, 5, 2, 128)
    packed = lax.all_to_all(packed, Z_ROW, 0, 0, tiled=True)
    spread = call(
        spread_kernel,
        shape((N_X, 512, 128), BF16),
        vmem(1),
        [pltpu.VMEM((N_ROW * N_Z * 10 + 8, 128), F32)],
    )(packed.reshape(N_ROW * N_Z * 10, 128))
    spread = lax.all_to_all(spread, "col_0", 0, 0, tiled=True)
    peers = N_ROW * N_X
    mixed, squares = call(
        product_kernel,
        (shape((peers, 32, 128), BF16), shape((N_Z, 1, 128), F32)),
        vmem(4),
        [pltpu.VMEM((2048 + 16, 128), F32)],
    )(spread, *points)
    squares = lax.all_to_all(squares, "col_1", 0, 0, tiled=True)
    mixed = call(
        carry_kernel,
        shape((peers * 34, 128), BF16),
        vmem(2),
        [pltpu.VMEM((peers * 34 + 8, 128), F32)],
    )(mixed, squares)
    mixed = lax.all_to_all(mixed.reshape(peers, 17, 2, 128), X_ROW, 0, 0, tiled=True)
    return call(
        place_kernel,
        shape((8, 16, WIDTH), F32),
        vmem(1),
        [
            pltpu.VMEM((peers * 34 + 8, 128), F32),
            pltpu.VMEM((15, 128 + 8, 128), F32),
            pltpu.VMEM((8, 8, WIDTH), F32),
            pltpu.VMEM((8, 8, WIDTH), F32),
            pltpu.SemaphoreType.DMA((2,)),
        ],
        pltpu.HBM,
    )(mixed.reshape(peers * 34, 128))


def solution(mesh):
    finer = Mesh(mesh.devices.reshape(8, 2, 4, 8), ROW + COL)
    in_specs = (P(ROW, COL), P(COL, ROW), P(), P(), P())
    return jax.shard_map(
        shards, mesh=finer, in_specs=in_specs, out_specs=P(None, COL, ROW), check_vma=False
    )
```
